128 devices in a mesh: ij: 8 (over z_hi, x), vir: 16 (over y, z_lo, core).
Axes of the slice: x: 4, y: 4, z: 4 (z_hi: 2, z_lo: 2; z = z_hi * 2 + z_lo), core: 2. Of those that a mesh axis runs over, the one named last changes fastest.
Arguments:
- amplitudes: float32 [16384, 32768], P('ij', 'vir'), may hold values from -6 to 6
- integrals: float32 [256, 128, 256], P(('vir', 'ij')), may hold values from -0.03125 to 0.03125
- block_mask: int32 [256, 2], P(('vir', 'ij')), may hold values 0 or 1
- partner: int32 [16384], P(('ij', 'vir')), may hold values from 0 to 16383, as said below
- occ_pair: float32 [16384], P(('ij', 'vir')), may hold values from -4 to -1
- vir_pair: float32 [256], replicated, may hold values from 0.5 to 6
Outputs:
- update: float32 [16384, 256], P(('ij', 'vir'))
The draws below stay inside these ranges and needn't reach their ends.
Inputs may be any that keep to these rules, and one draw needn't show every extreme that they name: partner is an involution without fixed points: partner[partner[k]] = k and partner[k] != k.
All inputs are finite; a program needn't handle non-finite values. No bound on the sum of `block_mask` on one device may be relied on, other than what follows from the above.
Results may differ from the reference program's by a relative error of at most 0.000078.
Values sent between devices are 32-bit elements; how exact they have to be, the bound alone decides.
No kernel may reach another device: no remote copies, remote signals or barrier semaphores. Data moves between devices by JAX's collectives and lax.ppermute only.
A program may use at most 128 MiB of HBM per device.

```python
import jax
import jax.numpy as jnp
from jax import lax

TILE = 128
AB = 256
IJ = 16384
NCD = 256
ABT = 2


def draw_partner(key, part):
    key = jax.random.fold_in(key, 7)
    order = jax.random.permutation(key, IJ).astype(jnp.int32)
    paired = order.reshape(IJ // 2, 2)
    swapped = paired[:, ::-1].reshape(IJ)
    return jnp.zeros((IJ,), jnp.int32).at[order].set(swapped)


def with_ends(array, key, least, top_value):
    longest = array.shape.index(max(array.shape))
    spots = []
    for shift in (0, 1):
        where = [jax.random.randint(jax.random.fold_in(key, axis), (), 0, length) for axis, length in enumerate(array.shape)]
        where[longest] = (where[longest] + shift) % array.shape[longest]
        spots.append(tuple(where))
    return array.at[spots[0]].set(least).at[spots[1]].set(top_value)


def level_of(own_key, dims, shards, low, high):
    loudness = 1.0
    for dim, parts in shards:
        draws = jax.random.uniform(jax.random.fold_in(jax.random.fold_in(own_key, 6), dim), (parts,), jnp.float32, low / len(shards), high / len(shards))
        loudness = loudness * jnp.repeat(jnp.exp(draws), dims[dim] // parts).reshape((-1,) + (1,) * (len(dims) - 1 - dim))
    return loudness


def bell_draw(own_key, shape, spread, most, split=(), dtype=jnp.bfloat16):
    entries = jax.random.normal(own_key, shape, jnp.float32) * spread
    if len(split) > 0:
        entries = level_of(own_key, shape, split, -0.22, 0.18) * entries
    return jnp.clip(entries, min=-most, max=most).astype(dtype)


def setup_inputs(seed: int = 0) -> dict:
    arg_keys = jax.random.split(jax.random.key(seed), 7)
    return {
        "amplitudes": bell_draw(arg_keys[0], (IJ, NCD * TILE), 1.0, 6.0, ((0, 8), (1, 16)), jnp.float32),
        "integrals": bell_draw(arg_keys[1], (NCD, TILE, AB), (NCD * TILE) ** -0.5, 0.03125, ((0, 128),), jnp.float32),
        "block_mask": with_ends((jax.random.randint(arg_keys[2], (NCD, ABT), 0, 4) < 3).astype(jnp.int32), jax.random.fold_in(arg_keys[2], 1), 0, 1),
        "partner": draw_partner(jax.random.fold_in(arg_keys[6], 71), 0),
        "occ_pair": jnp.clip(-4.0 + 3.0 * jax.random.uniform(arg_keys[4], (IJ,), jnp.float32) ** level_of(arg_keys[4], (IJ,), ((0, 128),), -0.2, 0.2), -4.0, -1.0),
        "vir_pair": jnp.clip(jax.random.uniform(arg_keys[5], (AB,), jnp.float32, 0.5, 6.0), 0.5, 6.0),
    }


def reference(amplitudes, integrals, block_mask, partner, occ_pair, vir_pair):
    tile_count = integrals.shape[0]
    tile_size = integrals.shape[1]
    ab_width = integrals.shape[2]
    tile_slots = ab_width // tile_size
    scaled = integrals.reshape(tile_count, tile_size, tile_slots, tile_size) * block_mask.astype(jnp.float32)[:, None, :, None]
    masked_v = scaled.reshape(tile_count * tile_size, ab_width)
    ladder = jnp.dot(amplitudes, masked_v, precision=lax.Precision.HIGHEST, preferred_element_type=jnp.float32)
    mirrored = jnp.take(ladder, partner, axis=0)
    denominator = vir_pair[None, :] - occ_pair[:, None]
    return (ladder - mirrored) / denominator
```

```python
import functools

import jax
import jax.numpy as jnp
from jax import lax
from jax.experimental import pallas as pl
from jax.experimental.pallas import tpu as pltpu
from jax.sharding import Mesh
from jax.sharding import PartitionSpec as P

SLOTS = 8
STRIDE = SLOTS + 1


def split_bf16(values):
    high = values.astype(jnp.bfloat16)
    low = (values - high.astype(jnp.float32)).astype(jnp.bfloat16)
    return high, low


def product_kernel(parts, first, *refs):
    _, *refs = refs
    pieces = sum(parts)
    lefts = refs[: len(parts)]
    rights = refs[len(parts) : len(parts) + pieces]
    total_in = None if first else refs[len(parts) + pieces]
    total_out = refs[-1]
    shape = total_out.shape
    rows = shape[1] * shape[2]
    total = None if first else total_in[...].reshape(rows, shape[3])
    at = 0
    for left, count in zip(lefts, parts):
        right = [rights[at + n][...] for n in range(count)]
        at += count
        right = right[0] if count == 1 else jnp.concatenate(right, axis=0)
        right_high, right_low = split_bf16(right)
        left_high, left_low = split_bf16(left[...].reshape(rows, right.shape[0]))
        dot = functools.partial(jnp.dot, preferred_element_type=jnp.float32)
        term = dot(left_high, right_low) + dot(left_low, right_high) + dot(left_high, right_high)
        total = term if total is None else total + term
    total_out[...] = total.reshape(shape)


def add_product(amps, places, groups, total, halves=(0, 1)):
    blocks, _, tile, _ = amps.shape
    width = groups[0][0].shape[-1]
    deep = sum(block.shape[0] for block in groups[0])
    run = 4
    parts = tuple(len(group) for group in groups)
    first = total is None
    half_count = len(halves)
    base = halves[0]

    def left_map(n):
        return lambda h, b, at: (b, at[h + base], 0, at[2 + n])

    in_specs = [pl.BlockSpec((run, None, tile, deep), left_map(n)) for n in range(len(groups))]
    operands = [amps] * len(groups)
    for group in groups:
        for block in group:
            in_specs.append(pl.BlockSpec(block.shape, lambda h, b, at: (0, 0)))
            operands.append(block)
    total_spec = pl.BlockSpec((1, run, tile, width), lambda h, b, at: (h, b, 0, 0))
    shape = (half_count, blocks, tile, width)
    aliases = {}
    if not first:
        in_specs.append(pl.BlockSpec((1, run, tile, width), lambda h, b, at: (h + base, b, 0, 0)))
        operands.append(total)
        if half_count == 2:
            aliases = {len(operands): 0}
    rows = half_count * blocks * tile
    return pl.pallas_call(
        functools.partial(product_kernel, parts, first),
        grid_spec=pltpu.PrefetchScalarGridSpec(
            num_scalar_prefetch=1,
            grid=(half_count, blocks // run),
            in_specs=in_specs,
            out_specs=total_spec,
        ),
        out_shape=jax.ShapeDtypeStruct(shape, jnp.float32),
        input_output_aliases=aliases,
        cost_estimate=pl.CostEstimate(
            flops=6 * rows * deep * width * len(groups),
            bytes_accessed=4 * rows * (deep * len(groups) + width),
            transcendentals=0,
        ),
        compiler_params=pltpu.CompilerParams(vmem_limit_bytes=40 * 2**20),
    )(places, *operands)


def pack_rows(own, place, out):
    half = own.shape[1] // 2
    for k in range(own.shape[0]):
        to = place[k]
        out[to, 0:1, :] = own[k : k + 1, :half]
        out[to, 1:2, :] = own[k : k + 1, half:]


def pack_kernel(place, most, partials, own, out):
    own[...] = jnp.sum(partials[...], axis=0)
    pack_rows(own, place, out)
    mark = jnp.broadcast_to(most[...], (2, most.shape[1]))

    def note(d, _):
        out[d * STRIDE + SLOTS] = mark
        return 0

    lax.fori_loop(0, out.shape[0] // STRIDE, note, 0, unroll=16)


def repack_kernel(place, own, out):
    pack_rows(own, place, out)


def unpack_kernel(place, got, own, scale, out, most, held):
    half = own.shape[1] // 2
    for k in range(own.shape[0]):
        at = place[k]
        held[k : k + 1, :half] = got[at, 0:1, :]
        held[k : k + 1, half:] = got[at, 1:2, :]
    worst = jnp.zeros(most.shape, jnp.float32)
    for d in range(got.shape[0] // STRIDE):
        worst = jnp.maximum(worst, got[d * STRIDE + SLOTS])
    most[...] = worst
    out[...] = (own[...] - held[...]) / scale[...]


def mend_kernel(place, got, own, scale, before, out):
    half = own.shape[1] // 2
    for k in range(own.shape[0]):
        at = place[k]
        row = slice(k, k + 1)
        for part, lanes in enumerate((slice(0, half), slice(half, 2 * half))):
            fresh = (own[row, lanes] - got[jnp.maximum(at, 0), part : part + 1, :]) / scale[row, lanes]
            out[row, lanes] = jnp.where(at >= 0, fresh, before[row, lanes])


SMEM = pl.BlockSpec(memory_space=pltpu.SMEM)
VMEM = pl.BlockSpec(memory_space=pltpu.VMEM)


def on_device(amplitudes, integrals, block_mask, partner, occ_pair, vir_pair):
    tiles, tile, width = integrals.shape
    slots = width // tile
    row_count = partner.shape[0]
    z_size, x_size, y_size, zl_size, core_size = (lax.axis_size(a) for a in ("zh", "x", "y", "zl", "c"))
    device_count = z_size * x_size * y_size * zl_size * core_size
    zh, x, core = lax.axis_index("zh"), lax.axis_index("x"), lax.axis_index("c")

    mask = jnp.repeat(block_mask.astype(jnp.float32), tile, axis=1)
    mine = (integrals * mask[:, None, :]).reshape(tiles * tile, width)
    cut = tiles * tile // 2

    def shift(block, by):
        return lax.ppermute(block, "x", [(n, (n + by) % x_size) for n in range(x_size)])

    up1 = shift(mine, 1)
    down1 = shift(mine, -1)
    across = lax.ppermute(mine, "zh", [(0, 1), (1, 0)])
    up2 = shift(up1[:cut], 1)
    down2 = shift(down1[cut:], -1)
    across_up1 = shift(across, 1)
    across_down1 = shift(across, -1)
    across_up2 = shift(across_up1[:cut], 1)
    across_down2 = shift(across_down1[cut:], -1)

    here, there = zh * x_size, (1 - zh) * x_size
    left, right, far = (x + x_size - 1) % x_size, (x + 1) % x_size, (x + 2) % x_size
    amps = amplitudes.reshape(y_size * zl_size, core_size, row_count, amplitudes.shape[1])

    def places(*columns):
        return jnp.stack([1 - core, core, *columns]).astype(jnp.int32)

    total = add_product(amps, places(here + x), [[mine]], None)
    total = add_product(
        amps,
        places(here + left, here + right, there + x),
        [[up1], [down1], [across]],
        total,
    )
    total = add_product(
        amps,
        places(here + far, there + left, there + right),
        [[up2, down2], [across_up1], [across_down1]],
        total,
    )
    last = [[across_up2, across_down2]]
    outgoing = add_product(amps, places(there + far), last, total, (0,))
    incoming = lax.ppermute(outgoing, "c", [(0, 1), (1, 0)])
    kept = add_product(amps, places(there + far), last, total, (1,))
    chip_sum = (kept + incoming)[0]
    partials = lax.all_to_all(chip_sum, ("y", "zl"), 0, 0, tiled=True)

    to = partner // row_count
    same = to[:, None] == to[None, :]
    index = jnp.arange(row_count, dtype=jnp.int32)
    send_rank = jnp.sum(same & (index[None, :] < index[:, None]), axis=1, dtype=jnp.int32)
    take_rank = jnp.sum(same & (partner[None, :] < partner[:, None]), axis=1, dtype=jnp.int32)
    longest = jnp.max(send_rank) + 1
    most = jnp.broadcast_to(longest.astype(jnp.float32), (1, width // 2))
    scale = vir_pair[None, :] - occ_pair[:, None]

    def send_place(turn):
        inside = send_rank // SLOTS == turn
        return to * STRIDE + jnp.where(inside, send_rank % SLOTS, SLOTS)

    packed = jax.ShapeDtypeStruct((device_count * STRIDE, 2, width // 2), jnp.float32)
    rows = jax.ShapeDtypeStruct((row_count, width), jnp.float32)
    everyone = ("zh", "x", "y", "zl", "c")
    own, outbox = pl.pallas_call(
        pack_kernel,
        in_specs=[SMEM, VMEM, VMEM],
        out_specs=[VMEM, VMEM],
        out_shape=[rows, packed],
    )(send_place(0), most, partials)
    inbox = lax.all_to_all(outbox, everyone, 0, 0, tiled=True)
    update, worst = pl.pallas_call(
        unpack_kernel,
        in_specs=[SMEM, VMEM, VMEM, VMEM],
        out_specs=[VMEM, VMEM],
        out_shape=[rows, jax.ShapeDtypeStruct((2, width // 2), jnp.float32)],
        scratch_shapes=[pltpu.VMEM((row_count, width), jnp.float32)],
    )(to * STRIDE + take_rank % SLOTS, inbox, own, scale)

    turns = (worst[0, 0].astype(jnp.int32) + SLOTS - 1) // SLOTS

    def more(state):
        return state[0] < turns

    def again(state):
        turn, before = state
        outbox = pl.pallas_call(
            repack_kernel, in_specs=[SMEM, VMEM], out_specs=VMEM, out_shape=packed
        )(send_place(turn), own)
        inbox = lax.all_to_all(outbox, everyone, 0, 0, tiled=True)
        place = jnp.where(take_rank // SLOTS == turn, to * STRIDE + take_rank % SLOTS, -1)
        after = pl.pallas_call(
            mend_kernel, in_specs=[SMEM, VMEM, VMEM, VMEM, VMEM], out_specs=VMEM, out_shape=rows
        )(place, inbox, own, scale, before)
        return turn + 1, after

    return lax.while_loop(more, again, (jnp.int32(1), update))[1]


def solution(mesh):
    fine = Mesh(mesh.devices.reshape(2, 4, 4, 2, 2), ("zh", "x", "y", "zl", "c"))
    ij, vir = ("zh", "x"), ("y", "zl", "c")
    in_specs = (
        P(ij, vir),
        P(vir + ij, None, None),
        P(vir + ij, None),
        P(ij + vir),
        P(ij + vir),
        P(),
    )
    return jax.shard_map(
        on_device, mesh=fine, in_specs=in_specs, out_specs=P(ij + vir, None), check_vma=False
    )
```

```python
import functools

import jax
import jax.numpy as jnp
from jax import lax
from jax.experimental import pallas as pl
from jax.experimental.pallas import tpu as pltpu
from jax.sharding import Mesh
from jax.sharding import PartitionSpec as P

SLOTS = 12
STRIDE = SLOTS + 1
STEP = 4
SMEM = pl.BlockSpec(memory_space=pltpu.SMEM)
VMEM = pl.BlockSpec(memory_space=pltpu.VMEM)
HBM = pl.BlockSpec(memory_space=pltpu.HBM)
SMALL = pltpu.CompilerParams(vmem_limit_bytes=12 * 2**20)


def in_vmem(array):
    return pltpu.with_memory_space_constraint(array, pltpu.VMEM)


def in_hbm(array):
    return pltpu.with_memory_space_constraint(array, pltpu.HBM)


def split_bf16(values):
    high = values.astype(jnp.bfloat16)
    low = (values - high.astype(jnp.float32)).astype(jnp.bfloat16)
    return high, low


def product_kernel(halves, count, at, places, left, *refs):
    blocks = refs[:count]
    totals, out = refs[count:]
    deep, width = blocks[0].shape
    runs, tile = left.shape[0] // STEP, left.shape[2]
    right = []
    for block in blocks:
        high, low = split_bf16(block[...])
        right += [low, high, high]
    right = jnp.concatenate(right, axis=0)
    for spot, half in enumerate(halves):
        for run in range(runs):
            rows = slice(run * STEP, (run + 1) * STEP)
            strips = []
            for n in range(count):
                columns = pl.ds(pl.multiple_of(places[at + n] * deep, deep), deep)
                strip = left[rows, places[half], :, columns].reshape(STEP * tile, deep)
                high, low = split_bf16(strip)
                strips += [high, low, high]
            term = jnp.dot(jnp.concatenate(strips, axis=1), right, preferred_element_type=jnp.float32)
            term = term.reshape(STEP, tile, width)
            out[spot, rows] = term + totals[half, rows]


def add_product(amps, places, at, blocks, totals, halves=(0, 1)):
    runs, _, tile, _ = amps.shape
    deep, width = blocks[0].shape
    operands = [places, amps, *(in_vmem(block) for block in blocks), totals]
    rows = len(halves) * runs * tile
    return pl.pallas_call(
        functools.partial(product_kernel, halves, len(blocks), at),
        in_specs=[SMEM] + [VMEM] * (len(operands) - 1),
        out_specs=VMEM,
        out_shape=pltpu.VMEM((len(halves), runs, tile, width), jnp.float32),
        input_output_aliases={len(operands) - 1: 0} if len(halves) == 2 else {},
        cost_estimate=pl.CostEstimate(
            flops=6 * rows * deep * width * len(blocks), bytes_accessed=4 * rows * width, transcendentals=0
        ),
        compiler_params=SMALL,
    )(*operands)


def load_kernel(places, block, far, near, out, arrived):
    deep, width = block.shape
    tile = far.shape[2]
    step = far.shape[0] // arrived.shape[0]
    copies = []
    for n in range(arrived.shape[0]):
        part = pl.ds(n * step, step)
        copies.append(pltpu.make_async_copy(far.at[part], near.at[part], arrived.at[n]))
        copies[-1].start()
    high, low = split_bf16(block[...])
    right = jnp.concatenate([low, high, high], axis=0)
    columns = pl.ds(pl.multiple_of(places[2] * deep, deep), deep)
    for n, copy in enumerate(copies):
        copy.wait()
        rows = slice(n * step, (n + 1) * step)
        strip = jnp.concatenate(
            [near[rows, places[half], :, columns].reshape(step * tile, deep) for half in range(2)]
        )
        high, low = split_bf16(strip)
        term = jnp.dot(
            jnp.concatenate([high, low, high], axis=1), right, preferred_element_type=jnp.float32
        ).reshape(2, step, tile, width)
        out[:, rows] = term


def load_and_start(amps, places, block):
    runs, cores, tile, _ = amps.shape
    deep, width = block.shape
    rows = runs * cores * tile
    return pl.pallas_call(
        load_kernel,
        in_specs=[SMEM, VMEM, HBM],
        out_specs=[VMEM, VMEM],
        out_shape=[
            pltpu.VMEM(amps.shape, jnp.float32),
            pltpu.VMEM((cores, runs, tile, width), jnp.float32),
        ],
        scratch_shapes=[pltpu.SemaphoreType.DMA((4,))],
        cost_estimate=pl.CostEstimate(
            flops=6 * rows * deep * width, bytes_accessed=4 * amps.size, transcendentals=0
        ),
        compiler_params=SMALL,
    )(places, in_vmem(block), in_hbm(amps))


def mask_kernel(mask, block, out, flags, held, arrived):
    copies = [
        pltpu.make_async_copy(mask, flags, arrived.at[0]),
        pltpu.make_async_copy(block, held, arrived.at[1]),
    ]
    for copy in copies:
        copy.start()
    for copy in copies:
        copy.wait()
    tiles, tile, width = block.shape
    for t in range(tiles):
        for a in range(mask.shape[1]):
            lanes = slice(a * tile, (a + 1) * tile)
            out[t * tile : (t + 1) * tile, lanes] = held[t, :, lanes] * flags[t, a].astype(jnp.float32)


def sum_kernel(partials, out):
    out[...] = jnp.sum(partials[...], axis=0)


def pack_kernel(place, most, own, other, out):
    rows = own.shape[0]
    half = own.shape[1] // 2
    for part, source in enumerate((own, other)):
        for k in range(rows):
            to = place[part * rows + k]
            out[to, 0:1, :] = source[k : k + 1, :half]
            out[to, 1:2, :] = source[k : k + 1, half:]
    mark = jnp.full((2, half), most[0].astype(jnp.float32))
    for d in range(out.shape[0] // STRIDE):
        out[d * STRIDE + SLOTS] = mark


def unpack_kernel(place, got, own, scale, out, turns, held):
    half = own.shape[1] // 2
    for k in range(own.shape[0]):
        at = place[k]
        held[k : k + 1, :half] = got[at, 0:1, :]
        held[k : k + 1, half:] = got[at, 1:2, :]
    worst = jnp.zeros((2, half), jnp.float32)
    for d in range(got.shape[0] // STRIDE):
        worst = jnp.maximum(worst, got[d * STRIDE + SLOTS])
    turns[0] = (jnp.max(worst).astype(jnp.int32) + SLOTS - 1) // SLOTS
    out[...] = (own[...] - held[...]) / scale[...]


def mend_kernel(place, got, own, scale, before, out):
    half = own.shape[1] // 2
    for k in range(own.shape[0]):
        at = place[k]
        row = slice(k, k + 1)
        for part, lanes in enumerate((slice(0, half), slice(half, 2 * half))):
            fresh = (own[row, lanes] - got[jnp.maximum(at, 0), part : part + 1, :]) / scale[row, lanes]
            out[row, lanes] = jnp.where(at >= 0, fresh, before[row, lanes])


def on_device(amplitudes, integrals, block_mask, partner, occ_pair, vir_pair):
    tiles, tile, width = integrals.shape
    row_count = partner.shape[0]
    z_size, x_size, y_size, zl_size, core_size = (lax.axis_size(a) for a in ("zh", "x", "y", "zl", "c"))
    device_count = z_size * x_size * y_size * zl_size * core_size
    zh, x, core = lax.axis_index("zh"), lax.axis_index("x"), lax.axis_index("c")

    mine = pl.pallas_call(
        mask_kernel,
        in_specs=[HBM, HBM],
        out_specs=VMEM,
        out_shape=pltpu.VMEM((tiles * tile, width), jnp.float32),
        scratch_shapes=[
            pltpu.SMEM(block_mask.shape, jnp.int32),
            pltpu.VMEM(integrals.shape, jnp.float32),
            pltpu.SemaphoreType.DMA((2,)),
        ],
        compiler_params=SMALL,
    )(in_hbm(block_mask), in_hbm(integrals))

    def shift(block, by):
        return lax.ppermute(block, "x", [(n, (n + by) % x_size) for n in range(x_size)])

    across = lax.ppermute(mine, "zh", [(0, 1), (1, 0)])
    up1 = shift(mine, 1)
    down1 = shift(mine, -1)
    across_down1 = shift(across, -1)
    up2 = shift(up1, 1)
    across_up1 = shift(across, 1)
    across_far = shift(across_down1, -1)

    def swap(array):
        return lax.ppermute(array, "c", [(0, 1), (1, 0)])

    here, there = zh * x_size, (1 - zh) * x_size
    left, right, far = (x + x_size - 1) % x_size, (x + 1) % x_size, (x + 2) % x_size
    amps = amplitudes.reshape(y_size * zl_size, core_size, row_count, amplitudes.shape[1])

    where = [1 - core, core, here + x, there + x, here + left, here + right, there + right]
    where += [here + far, there + left, there + far]
    slot = jnp.arange(len(where), dtype=jnp.int32)
    places = jnp.zeros((len(where),), jnp.int32)
    for n, place in enumerate(where):
        places = jnp.where(slot == n, place.astype(jnp.int32), places)

    amps, total = load_and_start(amps, places, mine)
    total = add_product(amps, places, 3, [across, up1, down1], total)
    total = add_product(amps, places, 6, [across_down1, up2, across_up1], total)
    outgoing = add_product(amps, places, 9, [across_far], total, (0,))
    incoming = swap(outgoing)
    kept = add_product(amps, places, 9, [across_far], total, (1,))
    chip_sum = (kept + incoming)[0]
    partials = lax.all_to_all(chip_sum, ("y", "zl"), 0, 0, tiled=True)

    rows = pltpu.VMEM((row_count, width), jnp.float32)
    own = pl.pallas_call(
        sum_kernel, in_specs=[VMEM], out_specs=VMEM, out_shape=rows, compiler_params=SMALL
    )(in_vmem(partials))
    other = swap(own)

    wanted = jnp.concatenate([partner, swap(partner)])
    to = wanted // row_count
    row = jnp.arange(row_count, dtype=jnp.int32)
    index = jnp.concatenate([core * row_count + row, (1 - core) * row_count + row])
    earlier = (to[:, None] == to[None, :]) & (index[None, :] < index[:, None])
    send_rank = jnp.sum(earlier, axis=1, dtype=jnp.int32)
    most = (jnp.max(send_rank) + 1).reshape(1)
    chip = partner // (row_count * core_size)
    before = (chip[:, None] == chip[None, :]) & (partner[None, :] < partner[:, None])
    take_rank = jnp.sum(before, axis=1, dtype=jnp.int32)
    scale = vir_pair[None, :] - occ_pair[:, None]

    def send_place(turn):
        inside = (send_rank // SLOTS == turn) & (to % core_size == core)
        return to // core_size * STRIDE + jnp.where(inside, send_rank % SLOTS, SLOTS)

    packed = pltpu.VMEM((device_count // core_size * STRIDE, 2, width // 2), jnp.float32)
    chips = ("zh", "x", "y", "zl")

    def exchange(turn):
        outbox = pl.pallas_call(
            pack_kernel,
            in_specs=[SMEM, SMEM, VMEM, VMEM],
            out_specs=VMEM,
            out_shape=packed,
            compiler_params=SMALL,
        )(send_place(turn), most, own, other)
        return in_vmem(lax.all_to_all(outbox, chips, 0, 0, tiled=True))

    update, turns = pl.pallas_call(
        unpack_kernel,
        in_specs=[SMEM, VMEM, VMEM, VMEM],
        out_specs=[VMEM, SMEM],
        out_shape=[rows, pltpu.SMEM((1,), jnp.int32)],
        scratch_shapes=[pltpu.VMEM((row_count, width), jnp.float32)],
        compiler_params=SMALL,
    )(chip * STRIDE + take_rank % SLOTS, exchange(0), own, scale)

    def more(state):
        return state[0] < turns[0]

    def again(state):
        turn, so_far = state
        place = jnp.where(take_rank // SLOTS == turn, chip * STRIDE + take_rank % SLOTS, -1)
        after = pl.pallas_call(
            mend_kernel,
            in_specs=[SMEM, VMEM, VMEM, VMEM, VMEM],
            out_specs=VMEM,
            out_shape=rows,
            compiler_params=SMALL,
        )(place, exchange(turn), own, scale, so_far)
        return turn + 1, after

    return lax.while_loop(more, again, (jnp.int32(1), update))[1]


def solution(mesh):
    fine = Mesh(mesh.devices.reshape(2, 4, 4, 2, 2), ("zh", "x", "y", "zl", "c"))
    ij, vir = ("zh", "x"), ("y", "zl", "c")
    in_specs = (
        P(ij, vir),
        P(vir + ij, None, None),
        P(vir + ij, None),
        P(ij + vir),
        P(ij + vir),
        P(),
    )
    return jax.shard_map(
        on_device, mesh=fine, in_specs=in_specs, out_specs=P(ij + vir, None), check_vma=False
    )
```

```python
import functools

import jax
import jax.numpy as jnp
from jax import lax
from jax.experimental import pallas as pl
from jax.experimental.pallas import tpu as pltpu
from jax.sharding import Mesh
from jax.sharding import PartitionSpec as P

SLOTS = 12
STRIDE = SLOTS + 1
SMEM = pl.BlockSpec(memory_space=pltpu.SMEM)
VMEM = pl.BlockSpec(memory_space=pltpu.VMEM)
HBM = pl.BlockSpec(memory_space=pltpu.HBM)
SMALL = pltpu.CompilerParams(vmem_limit_bytes=12 * 2**20)


def in_vmem(array):
    return pltpu.with_memory_space_constraint(array, pltpu.VMEM)


def in_hbm(array):
    return pltpu.with_memory_space_constraint(array, pltpu.HBM)


def split_bf16(values):
    high = values.astype(jnp.bfloat16)
    low = (values - high.astype(jnp.float32)).astype(jnp.bfloat16)
    return high, low


def halves_of(block):
    high, low = split_bf16(block)
    return [low, high, high]


def strips_of(rows, width):
    high, low = split_bf16(rows.reshape(-1, width))
    return [high, low, high]


def product(strips, right):
    return jnp.dot(jnp.concatenate(strips, axis=1), right, preferred_element_type=jnp.float32)


def columns_of(place, deep):
    return pl.ds(pl.multiple_of(place * deep, deep), deep)


def bring(far, near, side, arrived):
    step = far.shape[0] // arrived.shape[0]
    wide = near.shape[3]
    copies = []
    for n in range(arrived.shape[0]):
        part = pl.ds(n * step, step)
        source = far.at[part, :, :, columns_of(side, wide)]
        copies.append(pltpu.make_async_copy(source, near.at[part], arrived.at[n]))
        copies[-1].start()
    return step, copies


def both_cores(near, places, rows, column, deep):
    columns = columns_of(column, deep)
    return jnp.concatenate(
        [near[rows, places[half], :, columns].reshape(-1, deep) for half in range(2)]
    )


def first_kernel(places, block, far, near, out, arrived):
    deep, width = block.shape
    step, copies = bring(far, near, places[2], arrived)
    right = jnp.concatenate(halves_of(block[...]), axis=0)
    for n, copy in enumerate(copies):
        copy.wait()
        rows = slice(n * step, (n + 1) * step)
        strips = strips_of(both_cores(near, places, rows, places[4], deep), deep)
        out[:, rows] = product(strips, right).reshape(2, step, -1, width)


def second_kernel(places, here, left, right, across, totals, far, near, out, arrived):
    deep, width = across.shape
    step, copies = bring(far, near, places[3], arrived)
    sides = jnp.concatenate(halves_of(left[...]) + halves_of(right[...]), axis=0)
    for n in range(len(copies)):
        rows = slice(n * step, (n + 1) * step)
        strips = []
        for column in (places[5], places[6]):
            strips += strips_of(both_cores(here, places, rows, column, deep), deep)
        out[:, rows] = totals[:, rows] + product(strips, sides).reshape(2, step, -1, width)
    beyond = jnp.concatenate(halves_of(across[...]), axis=0)
    for n, copy in enumerate(copies):
        copy.wait()
        rows = slice(n * step, (n + 1) * step)
        strips = strips_of(both_cores(near, places, rows, places[4], deep), deep)
        out[:, rows] += product(strips, beyond).reshape(2, step, -1, width)


def last_kernel(half, places, here, there, far, across_left, across_right, across_far, totals, out):
    deep, width = far.shape
    blocks = (
        (here, places[7], far),
        (there, places[5], across_left),
        (there, places[6], across_right),
        (there, places[7], across_far),
    )
    right = jnp.concatenate(sum((halves_of(block[...]) for _, _, block in blocks), []), axis=0)
    step = 4
    for n in range(here.shape[0] // step):
        rows = slice(n * step, (n + 1) * step)
        strips = []
        for near, column, _ in blocks:
            strips += strips_of(near[rows, places[half], :, columns_of(column, deep)], deep)
        out[rows] = totals[half, rows] + product(strips, right).reshape(step, -1, width)


def call(kernel, operands, specs, results, scratch=(), aliases={}, flops=0):
    return pl.pallas_call(
        kernel,
        in_specs=specs,
        out_specs=[VMEM] * len(results),
        out_shape=[pltpu.VMEM(shape, jnp.float32) for shape in results],
        scratch_shapes=scratch,
        input_output_aliases=aliases,
        cost_estimate=pl.CostEstimate(flops=flops, bytes_accessed=2**20, transcendentals=0),
        compiler_params=SMALL,
    )(*operands)


def mask_kernel(mask, block, out, flags, held, arrived):
    copies = [
        pltpu.make_async_copy(mask, flags, arrived.at[0]),
        pltpu.make_async_copy(block, held, arrived.at[1]),
    ]
    for copy in copies:
        copy.start()
    for copy in copies:
        copy.wait()
    tiles, tile, width = block.shape
    for t in range(tiles):
        for a in range(mask.shape[1]):
            lanes = slice(a * tile, (a + 1) * tile)
            out[t * tile : (t + 1) * tile, lanes] = held[t, :, lanes] * flags[t, a].astype(jnp.float32)


def add_kernel(left, right, out):
    out[...] = left[...] + right[...]


def sum_kernel(partials, out):
    out[...] = jnp.sum(partials[...], axis=0)


def pack_kernel(place, most, own, other, out):
    rows = own.shape[0]
    half = own.shape[1] // 2
    for part, source in enumerate((own, other)):
        for k in range(rows):
            to = place[part * rows + k]
            out[to, 0:1, :] = source[k : k + 1, :half]
            out[to, 1:2, :] = source[k : k + 1, half:]
    mark = jnp.full((2, half), most[0].astype(jnp.float32))
    for d in range(out.shape[0] // STRIDE):
        out[d * STRIDE + SLOTS] = mark


def unpack_kernel(place, got, own, scale, out, turns, held):
    half = own.shape[1] // 2
    for k in range(own.shape[0]):
        at = place[k]
        held[k : k + 1, :half] = got[at, 0:1, :]
        held[k : k + 1, half:] = got[at, 1:2, :]
    worst = jnp.zeros((2, half), jnp.float32)
    for d in range(got.shape[0] // STRIDE):
        worst = jnp.maximum(worst, got[d * STRIDE + SLOTS])
    turns[0] = (jnp.max(worst).astype(jnp.int32) + SLOTS - 1) // SLOTS
    out[...] = (own[...] - held[...]) / scale[...]


def mend_kernel(place, got, own, scale, before, out):
    half = own.shape[1] // 2
    for k in range(own.shape[0]):
        at = place[k]
        row = slice(k, k + 1)
        for part, lanes in enumerate((slice(0, half), slice(half, 2 * half))):
            fresh = (own[row, lanes] - got[jnp.maximum(at, 0), part : part + 1, :]) / scale[row, lanes]
            out[row, lanes] = jnp.where(at >= 0, fresh, before[row, lanes])


def on_device(amplitudes, integrals, block_mask, partner, occ_pair, vir_pair):
    tiles, tile, width = integrals.shape
    row_count = partner.shape[0]
    z_size, x_size, y_size, zl_size, core_size = (lax.axis_size(a) for a in ("zh", "x", "y", "zl", "c"))
    device_count = z_size * x_size * y_size * zl_size * core_size
    zh, x, core = lax.axis_index("zh"), lax.axis_index("x"), lax.axis_index("c")

    mine = pl.pallas_call(
        mask_kernel,
        in_specs=[HBM, HBM],
        out_specs=VMEM,
        out_shape=pltpu.VMEM((tiles * tile, width), jnp.float32),
        scratch_shapes=[
            pltpu.SMEM(block_mask.shape, jnp.int32),
            pltpu.VMEM(integrals.shape, jnp.float32),
            pltpu.SemaphoreType.DMA((2,)),
        ],
        compiler_params=SMALL,
    )(in_hbm(block_mask), in_hbm(integrals))

    def shift(block, by):
        return lax.ppermute(block, "x", [(n, (n + by) % x_size) for n in range(x_size)])

    def cross(block):
        return lax.ppermute(block, "zh", [(0, 1), (1, 0)])

    def swap(array):
        return lax.ppermute(array, "c", [(0, 1), (1, 0)])

    amps = amplitudes.reshape(y_size * zl_size, core_size, row_count, amplitudes.shape[1])

    left, right, opposite = (x + x_size - 1) % x_size, (x + 1) % x_size, (x + 2) % x_size
    where = [1 - core, core, zh, 1 - zh, x, left, right, opposite]
    slot = jnp.arange(len(where), dtype=jnp.int32)
    places = jnp.zeros((len(where),), jnp.int32)
    for n, place in enumerate(where):
        places = jnp.where(slot == n, place.astype(jnp.int32), places)

    chunks = y_size * zl_size
    wide = amplitudes.shape[1] // z_size
    side = (chunks, core_size, row_count, wide)
    sums = (core_size, chunks, row_count, width)
    loads = [pltpu.SemaphoreType.DMA((4,))]
    work = 6 * core_size * chunks * row_count * width * tiles * tile

    across, up1, down1 = cross(mine), shift(mine, 1), shift(mine, -1)
    around = [(n, (1 - n // x_size) * x_size + (n + 2) % x_size) for n in range(2 * x_size)]
    across_far = lax.ppermute(mine, ("zh", "x"), around)
    here, total = call(
        first_kernel,
        [places, mine, in_hbm(amps)],
        [SMEM, VMEM, HBM],
        [side, sums],
        loads,
        flops=work,
    )
    across, up1, total = lax.optimization_barrier((across, up1, total))
    across_down1 = shift(across, -1)
    up2 = shift(up1, 1)
    across_up1 = cross(up1)
    there, total = call(
        second_kernel,
        [places, here, in_vmem(up1), in_vmem(down1), in_vmem(across), total, in_hbm(amps)],
        [SMEM, VMEM, VMEM, VMEM, VMEM, VMEM, HBM],
        [side, sums],
        loads,
        {5: 1},
        3 * work,
    )
    blocks = [in_vmem(block) for block in (up2, across_up1, across_down1, across_far)]

    def finish(half):
        (out,) = call(
            functools.partial(last_kernel, half),
            [places, here, there, *blocks, total],
            [SMEM] + [VMEM] * 7,
            [sums[1:]],
            flops=2 * work,
        )
        return out

    incoming = swap(finish(0))
    (chip_sum,) = call(add_kernel, [finish(1), in_vmem(incoming)], [VMEM, VMEM], [sums[1:]])
    partials = lax.all_to_all(chip_sum, ("y", "zl"), 0, 0, tiled=True)

    rows = pltpu.VMEM((row_count, width), jnp.float32)
    own = pl.pallas_call(
        sum_kernel, in_specs=[VMEM], out_specs=VMEM, out_shape=rows, compiler_params=SMALL
    )(in_vmem(partials))
    other = swap(own)

    wanted = jnp.concatenate([partner, swap(partner)])
    to = wanted // row_count
    row = jnp.arange(row_count, dtype=jnp.int32)
    index = jnp.concatenate([core * row_count + row, (1 - core) * row_count + row])
    earlier = (to[:, None] == to[None, :]) & (index[None, :] < index[:, None])
    send_rank = jnp.sum(earlier, axis=1, dtype=jnp.int32)
    most = (jnp.max(send_rank) + 1).reshape(1)
    chip = partner // (row_count * core_size)
    before = (chip[:, None] == chip[None, :]) & (partner[None, :] < partner[:, None])
    take_rank = jnp.sum(before, axis=1, dtype=jnp.int32)
    scale = vir_pair[None, :] - occ_pair[:, None]

    def send_place(turn):
        inside = (send_rank // SLOTS == turn) & (to % core_size == core)
        return to // core_size * STRIDE + jnp.where(inside, send_rank % SLOTS, SLOTS)

    packed = pltpu.VMEM((device_count // core_size * STRIDE, 2, width // 2), jnp.float32)
    chips = ("zh", "x", "y", "zl")

    def exchange(turn):
        outbox = pl.pallas_call(
            pack_kernel,
            in_specs=[SMEM, SMEM, VMEM, VMEM],
            out_specs=VMEM,
            out_shape=packed,
            compiler_params=SMALL,
        )(send_place(turn), most, own, other)
        return in_vmem(lax.all_to_all(outbox, chips, 0, 0, tiled=True))

    update, turns = pl.pallas_call(
        unpack_kernel,
        in_specs=[SMEM, VMEM, VMEM, VMEM],
        out_specs=[VMEM, SMEM],
        out_shape=[rows, pltpu.SMEM((1,), jnp.int32)],
        scratch_shapes=[pltpu.VMEM((row_count, width), jnp.float32)],
        compiler_params=SMALL,
    )(chip * STRIDE + take_rank % SLOTS, exchange(0), own, scale)

    def more(state):
        return state[0] < turns[0]

    def again(state):
        turn, so_far = state
        place = jnp.where(take_rank // SLOTS == turn, chip * STRIDE + take_rank % SLOTS, -1)
        after = pl.pallas_call(
            mend_kernel,
            in_specs=[SMEM, VMEM, VMEM, VMEM, VMEM],
            out_specs=VMEM,
            out_shape=rows,
            compiler_params=SMALL,
        )(place, exchange(turn), own, scale, so_far)
        return turn + 1, after

    return lax.while_loop(more, again, (jnp.int32(1), update))[1]


def solution(mesh):
    fine = Mesh(mesh.devices.reshape(2, 4, 4, 2, 2), ("zh", "x", "y", "zl", "c"))
    ij, vir = ("zh", "x"), ("y", "zl", "c")
    in_specs = (
        P(ij, vir),
        P(vir + ij, None, None),
        P(vir + ij, None),
        P(ij + vir),
        P(ij + vir),
        P(),
    )
    return jax.shard_map(
        on_device, mesh=fine, in_specs=in_specs, out_specs=P(ij + vir, None), check_vma=False
    )
```

```python
import functools

import jax
import jax.numpy as jnp
from jax import lax
from jax.experimental import pallas as pl
from jax.experimental.pallas import tpu as pltpu
from jax.sharding import Mesh
from jax.sharding import PartitionSpec as P

SLOTS = 12
STRIDE = SLOTS + 1
SMEM = pl.BlockSpec(memory_space=pltpu.SMEM)
VMEM = pl.BlockSpec(memory_space=pltpu.VMEM)
HBM = pl.BlockSpec(memory_space=pltpu.HBM)
SMALL = pltpu.CompilerParams(vmem_limit_bytes=12 * 2**20)


def in_vmem(array):
    return pltpu.with_memory_space_constraint(array, pltpu.VMEM)


def in_hbm(array):
    return pltpu.with_memory_space_constraint(array, pltpu.HBM)


def split_bf16(values):
    high = values.astype(jnp.bfloat16)
    low = (values - high.astype(jnp.float32)).astype(jnp.bfloat16)
    return high, low


def halves_of(block):
    high, low = split_bf16(block)
    return [low, high, high]


def strips_of(rows, width):
    high, low = split_bf16(rows.reshape(-1, width))
    return [high, low, high]


def product(strips, right):
    return jnp.dot(jnp.concatenate(strips, axis=1), right, preferred_element_type=jnp.float32)


def columns_of(place, deep):
    return pl.ds(pl.multiple_of(place * deep, deep), deep)


def bring(far, near, side, arrived):
    step = far.shape[0] // arrived.shape[0]
    wide = near.shape[3]
    copies = []
    for n in range(arrived.shape[0]):
        part = pl.ds(n * step, step)
        source = far.at[part, :, :, columns_of(side, wide)]
        copies.append(pltpu.make_async_copy(source, near.at[part], arrived.at[n]))
        copies[-1].start()
    return step, copies


def both_cores(near, places, rows, column, deep):
    columns = columns_of(column, deep)
    return jnp.concatenate(
        [near[rows, places[half], :, columns].reshape(-1, deep) for half in range(2)]
    )


def first_kernel(places, block, far, near, out, arrived):
    deep, width = block.shape
    step, copies = bring(far, near, places[2], arrived)
    right = jnp.concatenate(halves_of(block[...]), axis=0)
    for n, copy in enumerate(copies):
        copy.wait()
        rows = slice(n * step, (n + 1) * step)
        strips = strips_of(both_cores(near, places, rows, places[4], deep), deep)
        out[:, rows] = product(strips, right).reshape(2, step, -1, width)


def second_kernel(places, here, left, right, across, totals, far, near, out, arrived):
    deep, width = across.shape
    step, copies = bring(far, near, places[3], arrived)
    sides = jnp.concatenate(halves_of(left[...]) + halves_of(right[...]), axis=0)
    for n in range(len(copies)):
        rows = slice(n * step, (n + 1) * step)
        strips = []
        for column in (places[5], places[6]):
            strips += strips_of(both_cores(here, places, rows, column, deep), deep)
        out[:, rows] = totals[:, rows] + product(strips, sides).reshape(2, step, -1, width)
    beyond = jnp.concatenate(halves_of(across[...]), axis=0)
    for n, copy in enumerate(copies):
        copy.wait()
        rows = slice(n * step, (n + 1) * step)
        strips = strips_of(both_cores(near, places, rows, places[4], deep), deep)
        out[:, rows] += product(strips, beyond).reshape(2, step, -1, width)


def last_kernel(half, places, here, there, far, across_left, across_right, across_far, totals, out):
    deep, width = far.shape
    blocks = (
        (here, places[7], far),
        (there, places[5], across_left),
        (there, places[6], across_right),
        (there, places[7], across_far),
    )
    right = jnp.concatenate(sum((halves_of(block[...]) for _, _, block in blocks), []), axis=0)
    step = 4
    for n in range(here.shape[0] // step):
        rows = slice(n * step, (n + 1) * step)
        strips = []
        for near, column, _ in blocks:
            strips += strips_of(near[rows, places[half], :, columns_of(column, deep)], deep)
        out[rows] = totals[half, rows] + product(strips, right).reshape(step, -1, width)


def call(kernel, operands, specs, results, scratch=(), aliases={}, flops=0):
    return pl.pallas_call(
        kernel,
        in_specs=specs,
        out_specs=[VMEM] * len(results),
        out_shape=[pltpu.VMEM(shape, jnp.float32) for shape in results],
        scratch_shapes=scratch,
        input_output_aliases=aliases,
        cost_estimate=pl.CostEstimate(flops=flops, bytes_accessed=2**20, transcendentals=0),
        compiler_params=SMALL,
    )(*operands)


def mask_kernel(mask, block, out, flags, held, arrived):
    copies = [
        pltpu.make_async_copy(mask, flags, arrived.at[0]),
        pltpu.make_async_copy(block, held, arrived.at[1]),
    ]
    for copy in copies:
        copy.start()
    for copy in copies:
        copy.wait()
    tiles, tile, width = block.shape
    for t in range(tiles):
        for a in range(mask.shape[1]):
            lanes = slice(a * tile, (a + 1) * tile)
            out[t * tile : (t + 1) * tile, lanes] = held[t, :, lanes] * flags[t, a].astype(jnp.float32)


def add_kernel(places, left, right, *outs):
    for n, out in enumerate(outs):
        out[...] = left[places[8 + n]] + right[places[8 + n]]


def sum_kernel(*refs):
    *parts, out = refs
    out[...] = sum(part[...] for part in parts)


def pack_kernel(own_place, other_place, most, own, other, out):
    rows = own.shape[0]
    half = own.shape[1] // 2
    for place, source in ((own_place, own), (other_place, other)):
        for k in range(rows):
            to = place[k]
            out[to, 0:1, :] = source[k : k + 1, :half]
            out[to, 1:2, :] = source[k : k + 1, half:]
    mark = jnp.full((2, half), most[0].astype(jnp.float32))
    for d in range(out.shape[0] // STRIDE):
        out[d * STRIDE + SLOTS] = mark


def unpack_kernel(place, got, own, scale, out, turns, held):
    half = own.shape[1] // 2
    for k in range(own.shape[0]):
        at = place[k]
        held[k : k + 1, :half] = got[at, 0:1, :]
        held[k : k + 1, half:] = got[at, 1:2, :]
    worst = jnp.zeros((2, half), jnp.float32)
    for d in range(got.shape[0] // STRIDE):
        worst = jnp.maximum(worst, got[d * STRIDE + SLOTS])
    turns[0] = (jnp.max(worst).astype(jnp.int32) + SLOTS - 1) // SLOTS
    out[...] = (own[...] - held[...]) / scale[...]


def mend_kernel(place, got, own, scale, before, out):
    half = own.shape[1] // 2
    for k in range(own.shape[0]):
        at = place[k]
        row = slice(k, k + 1)
        for part, lanes in enumerate((slice(0, half), slice(half, 2 * half))):
            fresh = (own[row, lanes] - got[jnp.maximum(at, 0), part : part + 1, :]) / scale[row, lanes]
            out[row, lanes] = jnp.where(at >= 0, fresh, before[row, lanes])


def on_device(amplitudes, integrals, block_mask, partner, occ_pair, vir_pair):
    tiles, tile, width = integrals.shape
    row_count = partner.shape[0]
    z_size, x_size, y_size, zl_size, core_size = (lax.axis_size(a) for a in ("zh", "x", "y", "zl", "c"))
    device_count = z_size * x_size * y_size * zl_size * core_size
    zh, x, core = lax.axis_index("zh"), lax.axis_index("x"), lax.axis_index("c")

    mine = pl.pallas_call(
        mask_kernel,
        in_specs=[HBM, HBM],
        out_specs=VMEM,
        out_shape=pltpu.VMEM((tiles * tile, width), jnp.float32),
        scratch_shapes=[
            pltpu.SMEM(block_mask.shape, jnp.int32),
            pltpu.VMEM(integrals.shape, jnp.float32),
            pltpu.SemaphoreType.DMA((2,)),
        ],
        compiler_params=SMALL,
    )(in_hbm(block_mask), in_hbm(integrals))

    def shift(block, by):
        return lax.ppermute(block, "x", [(n, (n + by) % x_size) for n in range(x_size)])

    def cross(block):
        return lax.ppermute(block, "zh", [(0, 1), (1, 0)])

    def swap(array):
        return lax.ppermute(array, "c", [(0, 1), (1, 0)])

    amps = amplitudes.reshape(y_size * zl_size, core_size, row_count, amplitudes.shape[1])

    left, right, opposite = (x + x_size - 1) % x_size, (x + 1) % x_size, (x + 2) % x_size
    where = [1 - core, core, zh, 1 - zh, x, left, right, opposite]
    y, zl = lax.axis_index("y"), lax.axis_index("zl")
    moves = [(2, 1), (2, 0), (1, 1), (3, 1), (1, 0), (3, 0), (0, 1), (0, 0)]
    where += [(y + up) % y_size * zl_size + (zl + over) % zl_size for up, over in moves]
    slot = jnp.arange(len(where), dtype=jnp.int32)
    places = jnp.zeros((len(where),), jnp.int32)
    for n, place in enumerate(where):
        places = jnp.where(slot == n, place.astype(jnp.int32), places)

    chunks = y_size * zl_size
    wide = amplitudes.shape[1] // z_size
    side = (chunks, core_size, row_count, wide)
    sums = (core_size, chunks, row_count, width)
    loads = [pltpu.SemaphoreType.DMA((4,))]
    work = 6 * core_size * chunks * row_count * width * tiles * tile

    across, up1, down1 = cross(mine), shift(mine, 1), shift(mine, -1)
    around = [(n, (1 - n // x_size) * x_size + (n + 2) % x_size) for n in range(2 * x_size)]
    across_far = lax.ppermute(mine, ("zh", "x"), around)
    here, total = call(
        first_kernel,
        [places, mine, in_hbm(amps)],
        [SMEM, VMEM, HBM],
        [side, sums],
        loads,
        flops=work,
    )
    across, up1, total = lax.optimization_barrier((across, up1, total))
    across_down1 = shift(across, -1)
    up2 = shift(up1, 1)
    across_up1 = cross(up1)
    there, total = call(
        second_kernel,
        [places, here, in_vmem(up1), in_vmem(down1), in_vmem(across), total, in_hbm(amps)],
        [SMEM, VMEM, VMEM, VMEM, VMEM, VMEM, HBM],
        [side, sums],
        loads,
        {5: 1},
        3 * work,
    )
    blocks = [in_vmem(block) for block in (up2, across_up1, across_down1, across_far)]

    def finish(half):
        (out,) = call(
            functools.partial(last_kernel, half),
            [places, here, there, *blocks, total],
            [SMEM] + [VMEM] * 7,
            [sums[1:]],
            flops=2 * work,
        )
        return out

    incoming = swap(finish(0))
    parts = call(
        add_kernel,
        [places, finish(1), in_vmem(incoming)],
        [SMEM, VMEM, VMEM],
        [sums[2:]] * len(moves),
    )

    *parts, partner, core = lax.optimization_barrier((*parts, partner, core))

    def send(part, move):
        up, over = move
        pairs = [
            (a * zl_size + b, (a + up) % y_size * zl_size + (b + over) % zl_size)
            for a in range(y_size)
            for b in range(zl_size)
        ]
        return in_vmem(lax.ppermute(part, ("y", "zl"), pairs))

    partials = [send(part, move) for part, move in zip(parts[:-1], moves)] + [parts[-1]]

    rows = pltpu.VMEM((row_count, width), jnp.float32)
    own = pl.pallas_call(
        sum_kernel,
        in_specs=[VMEM] * len(partials),
        out_specs=VMEM,
        out_shape=rows,
        compiler_params=SMALL,
    )(*partials)
    other = swap(own)

    sibling = swap(partner)
    row = jnp.arange(row_count, dtype=jnp.int32)

    def rank(wanted, others, others_first):
        to, beside = wanted // row_count, others // row_count
        earlier = (to[:, None] == to[None, :]) & (row[None, :] < row[:, None])
        also = (to[:, None] == beside[None, :]) & others_first
        return jnp.sum(earlier.astype(jnp.int32) + also.astype(jnp.int32), axis=1)

    ranks = (rank(partner, sibling, core == 1), rank(sibling, partner, core == 0))
    most = (jnp.maximum(jnp.max(ranks[0]), jnp.max(ranks[1])) + 1).reshape(1)
    chip = partner // (row_count * core_size)
    before = (chip[:, None] == chip[None, :]) & (partner[None, :] < partner[:, None])
    take_rank = jnp.sum(before, axis=1, dtype=jnp.int32)
    scale = vir_pair[None, :] - occ_pair[:, None]

    def send_place(wanted, rank, turn):
        to = wanted // row_count
        inside = (rank // SLOTS == turn) & (to % core_size == core)
        return to // core_size * STRIDE + jnp.where(inside, rank % SLOTS, SLOTS)

    packed = pltpu.VMEM((device_count // core_size * STRIDE, 2, width // 2), jnp.float32)
    chips = ("zh", "x", "y", "zl")

    def exchange(turn):
        outbox = pl.pallas_call(
            pack_kernel,
            in_specs=[SMEM, SMEM, SMEM, VMEM, VMEM],
            out_specs=VMEM,
            out_shape=packed,
            compiler_params=SMALL,
        )(send_place(partner, ranks[0], turn), send_place(sibling, ranks[1], turn), most, own, other)
        return in_vmem(lax.all_to_all(outbox, chips, 0, 0, tiled=True))

    update, turns = pl.pallas_call(
        unpack_kernel,
        in_specs=[SMEM, VMEM, VMEM, VMEM],
        out_specs=[VMEM, SMEM],
        out_shape=[rows, pltpu.SMEM((1,), jnp.int32)],
        scratch_shapes=[pltpu.VMEM((row_count, width), jnp.float32)],
        compiler_params=SMALL,
    )(chip * STRIDE + take_rank % SLOTS, exchange(0), own, scale)

    def more(state):
        return state[0] < turns[0]

    def again(state):
        turn, so_far = state
        place = jnp.where(take_rank // SLOTS == turn, chip * STRIDE + take_rank % SLOTS, -1)
        after = pl.pallas_call(
            mend_kernel,
            in_specs=[SMEM, VMEM, VMEM, VMEM, VMEM],
            out_specs=VMEM,
            out_shape=rows,
            compiler_params=SMALL,
        )(place, exchange(turn), own, scale, so_far)
        return turn + 1, after

    return lax.while_loop(more, again, (jnp.int32(1), update))[1]


def solution(mesh):
    fine = Mesh(mesh.devices.reshape(2, 4, 4, 2, 2), ("zh", "x", "y", "zl", "c"))
    ij, vir = ("zh", "x"), ("y", "zl", "c")
    in_specs = (
        P(ij, vir),
        P(vir + ij, None, None),
        P(vir + ij, None),
        P(ij + vir),
        P(ij + vir),
        P(),
    )
    return jax.shard_map(
        on_device, mesh=fine, in_specs=in_specs, out_specs=P(ij + vir, None), check_vma=False
    )
```

```python
import functools

import jax
import jax.numpy as jnp
from jax import lax
from jax.experimental import pallas as pl
from jax.experimental.pallas import tpu as pltpu
from jax.sharding import Mesh
from jax.sharding import PartitionSpec as P

SLOTS = 12
STRIDE = SLOTS + 1
SMEM = pl.BlockSpec(memory_space=pltpu.SMEM)
VMEM = pl.BlockSpec(memory_space=pltpu.VMEM)
HBM = pl.BlockSpec(memory_space=pltpu.HBM)
SMALL = pltpu.CompilerParams(vmem_limit_bytes=12 * 2**20)


def in_vmem(array):
    return pltpu.with_memory_space_constraint(array, pltpu.VMEM)


def in_hbm(array):
    return pltpu.with_memory_space_constraint(array, pltpu.HBM)


def split_bf16(values):
    high = values.astype(jnp.bfloat16)
    low = (values - high.astype(jnp.float32)).astype(jnp.bfloat16)
    return high, low


def halves_of(block):
    high, low = split_bf16(block)
    return [low, high, high]


def strips_of(rows, width):
    high, low = split_bf16(rows.reshape(-1, width))
    return [high, low, high]


def product(strips, right):
    return jnp.dot(jnp.concatenate(strips, axis=1), right, preferred_element_type=jnp.float32)


def columns_of(place, deep):
    return pl.ds(pl.multiple_of(place * deep, deep), deep)


def bring(far, near, side, arrived):
    step = far.shape[0] // arrived.shape[0]
    wide = near.shape[3]
    copies = []
    for n in range(arrived.shape[0]):
        part = pl.ds(n * step, step)
        source = far.at[part, :, :, columns_of(side, wide)]
        copies.append(pltpu.make_async_copy(source, near.at[part], arrived.at[n]))
        copies[-1].start()
    return step, copies


def both_cores(near, places, rows, column, deep):
    columns = columns_of(column, deep)
    return jnp.concatenate(
        [near[rows, places[half], :, columns].reshape(-1, deep) for half in range(2)]
    )


def first_kernel(places, block, far, near, out, arrived):
    deep, width = block.shape
    step, copies = bring(far, near, places[2], arrived)
    right = jnp.concatenate(halves_of(block[...]), axis=0)
    for n, copy in enumerate(copies):
        copy.wait()
        rows = slice(n * step, (n + 1) * step)
        strips = strips_of(both_cores(near, places, rows, places[4], deep), deep)
        out[:, rows] = product(strips, right).reshape(2, step, -1, width)


def second_kernel(places, here, left, right, across, totals, far, near, out, arrived):
    deep, width = across.shape
    step, copies = bring(far, near, places[3], arrived)
    sides = jnp.concatenate(halves_of(left[...]) + halves_of(right[...]), axis=0)
    for n in range(len(copies)):
        rows = slice(n * step, (n + 1) * step)
        strips = []
        for column in (places[5], places[6]):
            strips += strips_of(both_cores(here, places, rows, column, deep), deep)
        out[:, rows] = totals[:, rows] + product(strips, sides).reshape(2, step, -1, width)
    beyond = jnp.concatenate(halves_of(across[...]), axis=0)
    for n, copy in enumerate(copies):
        copy.wait()
        rows = slice(n * step, (n + 1) * step)
        strips = strips_of(both_cores(near, places, rows, places[4], deep), deep)
        out[:, rows] += product(strips, beyond).reshape(2, step, -1, width)


def last_kernel(half, places, here, there, far, across_left, across_right, across_far, totals, out):
    deep, width = far.shape
    blocks = (
        (here, places[7], far),
        (there, places[5], across_left),
        (there, places[6], across_right),
        (there, places[7], across_far),
    )
    right = jnp.concatenate(sum((halves_of(block[...]) for _, _, block in blocks), []), axis=0)
    step = 4
    for n in range(here.shape[0] // step):
        rows = slice(n * step, (n + 1) * step)
        strips = []
        for near, column, _ in blocks:
            strips += strips_of(near[rows, places[half], :, columns_of(column, deep)], deep)
        out[rows] = totals[half, rows] + product(strips, right).reshape(step, -1, width)


def call(kernel, operands, specs, results, scratch=(), aliases={}, flops=0):
    return pl.pallas_call(
        kernel,
        in_specs=specs,
        out_specs=[VMEM] * len(results),
        out_shape=[pltpu.VMEM(shape, jnp.float32) for shape in results],
        scratch_shapes=scratch,
        input_output_aliases=aliases,
        cost_estimate=pl.CostEstimate(flops=flops, bytes_accessed=2**20, transcendentals=0),
        compiler_params=SMALL,
    )(*operands)


def mask_kernel(mask, block, out, flags, held, arrived):
    copies = [
        pltpu.make_async_copy(mask, flags, arrived.at[0]),
        pltpu.make_async_copy(block, held, arrived.at[1]),
    ]
    for copy in copies:
        copy.start()
    for copy in copies:
        copy.wait()
    tiles, tile, width = block.shape
    for t in range(tiles):
        for a in range(mask.shape[1]):
            lanes = slice(a * tile, (a + 1) * tile)
            out[t * tile : (t + 1) * tile, lanes] = held[t, :, lanes] * flags[t, a].astype(jnp.float32)


def add_kernel(places, left, right, *outs):
    for n, out in enumerate(outs):
        out[...] = left[places[8 + n]] + right[places[8 + n]]


def sum_kernel(*refs):
    *parts, out = refs
    out[...] = sum(part[...] for part in parts)


def pack_kernel(own_place, other_place, most, own, other, out):
    rows = own.shape[0]
    half = own.shape[1] // 2
    for place, source in ((own_place, own), (other_place, other)):
        for k in range(rows):
            to = place[k]
            out[to, 0:1, :] = source[k : k + 1, :half]
            out[to, 1:2, :] = source[k : k + 1, half:]
    mark = jnp.full((2, half), most[0].astype(jnp.float32))
    for d in range(out.shape[0] // STRIDE):
        out[d * STRIDE + SLOTS] = mark


def unpack_kernel(place, got, own, scale, out, turns, held):
    half = own.shape[1] // 2
    for k in range(own.shape[0]):
        at = place[k]
        held[k : k + 1, :half] = got[at, 0:1, :]
        held[k : k + 1, half:] = got[at, 1:2, :]
    worst = jnp.zeros((2, half), jnp.float32)
    for d in range(got.shape[0] // STRIDE):
        worst = jnp.maximum(worst, got[d * STRIDE + SLOTS])
    turns[0] = (jnp.max(worst).astype(jnp.int32) + SLOTS - 1) // SLOTS
    out[...] = (own[...] - held[...]) / scale[...]


def mend_kernel(place, got, own, scale, before, out):
    half = own.shape[1] // 2
    for k in range(own.shape[0]):
        at = place[k]
        row = slice(k, k + 1)
        for part, lanes in enumerate((slice(0, half), slice(half, 2 * half))):
            fresh = (own[row, lanes] - got[jnp.maximum(at, 0), part : part + 1, :]) / scale[row, lanes]
            out[row, lanes] = jnp.where(at >= 0, fresh, before[row, lanes])


def on_device(amplitudes, integrals, block_mask, partner, occ_pair, vir_pair):
    tiles, tile, width = integrals.shape
    row_count = partner.shape[0]
    z_size, x_size, y_size, zl_size, core_size = (lax.axis_size(a) for a in ("zh", "x", "y", "zl", "c"))
    device_count = z_size * x_size * y_size * zl_size * core_size
    zh, x, core = lax.axis_index("zh"), lax.axis_index("x"), lax.axis_index("c")

    mine = pl.pallas_call(
        mask_kernel,
        in_specs=[HBM, HBM],
        out_specs=VMEM,
        out_shape=pltpu.VMEM((tiles * tile, width), jnp.float32),
        scratch_shapes=[
            pltpu.SMEM(block_mask.shape, jnp.int32),
            pltpu.VMEM(integrals.shape, jnp.float32),
            pltpu.SemaphoreType.DMA((2,)),
        ],
        compiler_params=SMALL,
    )(in_hbm(block_mask), in_hbm(integrals))

    def shift(block, by):
        return lax.ppermute(block, "x", [(n, (n + by) % x_size) for n in range(x_size)])

    def cross(block):
        return lax.ppermute(block, "zh", [(0, 1), (1, 0)])

    def swap(array):
        return lax.ppermute(array, "c", [(0, 1), (1, 0)])

    amps = amplitudes.reshape(y_size * zl_size, core_size, row_count, amplitudes.shape[1])

    left, right, opposite = (x + x_size - 1) % x_size, (x + 1) % x_size, (x + 2) % x_size
    where = [1 - core, core, zh, 1 - zh, x, left, right, opposite]
    y, zl = lax.axis_index("y"), lax.axis_index("zl")
    moves = [(1, 1), (3, 1), (2, 1), (2, 0), (0, 1), (1, 0), (3, 0), (0, 0)]
    where += [(y + up) % y_size * zl_size + (zl + over) % zl_size for up, over in moves]
    slot = jnp.arange(len(where), dtype=jnp.int32)
    places = jnp.zeros((len(where),), jnp.int32)
    for n, place in enumerate(where):
        places = jnp.where(slot == n, place.astype(jnp.int32), places)

    chunks = y_size * zl_size
    wide = amplitudes.shape[1] // z_size
    side = (chunks, core_size, row_count, wide)
    sums = (core_size, chunks, row_count, width)
    loads = [pltpu.SemaphoreType.DMA((4,))]
    work = 6 * core_size * chunks * row_count * width * tiles * tile

    across, up1, down1 = cross(mine), shift(mine, 1), shift(mine, -1)
    around = [(n, (1 - n // x_size) * x_size + (n + 2) % x_size) for n in range(2 * x_size)]
    across_far = lax.ppermute(mine, ("zh", "x"), around)
    here, total = call(
        first_kernel,
        [places, mine, in_hbm(amps)],
        [SMEM, VMEM, HBM],
        [side, sums],
        loads,
        flops=work,
    )
    across, up1, total = lax.optimization_barrier((across, up1, total))
    across_down1 = shift(across, -1)
    up2 = shift(up1, 1)
    across_up1 = cross(up1)
    there, total = call(
        second_kernel,
        [places, here, in_vmem(up1), in_vmem(down1), in_vmem(across), total, in_hbm(amps)],
        [SMEM, VMEM, VMEM, VMEM, VMEM, VMEM, HBM],
        [side, sums],
        loads,
        {5: 1},
        3 * work,
    )
    blocks = [in_vmem(block) for block in (up2, across_up1, across_down1, across_far)]

    def finish(half):
        (out,) = call(
            functools.partial(last_kernel, half),
            [places, here, there, *blocks, total],
            [SMEM] + [VMEM] * 7,
            [sums[1:]],
            flops=2 * work,
        )
        return out

    incoming = swap(finish(0))
    parts = call(
        add_kernel,
        [places, finish(1), in_vmem(incoming)],
        [SMEM, VMEM, VMEM],
        [sums[2:]] * len(moves),
    )

    def send(part, move):
        up, over = move
        pairs = [
            (a * zl_size + b, (a + up) % y_size * zl_size + (b + over) % zl_size)
            for a in range(y_size)
            for b in range(zl_size)
        ]
        return in_vmem(lax.ppermute(part, ("y", "zl"), pairs))

    partials = [send(part, move) for part, move in zip(parts[:-1], moves)] + [parts[-1]]
    partials[0], partner, core = lax.optimization_barrier((partials[0], partner, core))

    rows = pltpu.VMEM((row_count, width), jnp.float32)
    own = pl.pallas_call(
        sum_kernel,
        in_specs=[VMEM] * len(partials),
        out_specs=VMEM,
        out_shape=rows,
        compiler_params=SMALL,
    )(*partials)
    other = swap(own)

    sibling = swap(partner)
    row = jnp.arange(row_count, dtype=jnp.int32)

    def rank(wanted, others, others_first):
        to, beside = wanted // row_count, others // row_count
        earlier = (to[:, None] == to[None, :]) & (row[None, :] < row[:, None])
        also = (to[:, None] == beside[None, :]) & others_first
        return jnp.sum(earlier.astype(jnp.int32) + also.astype(jnp.int32), axis=1)

    ranks = (rank(partner, sibling, core == 1), rank(sibling, partner, core == 0))
    most = (jnp.maximum(jnp.max(ranks[0]), jnp.max(ranks[1])) + 1).reshape(1)
    chip = partner // (row_count * core_size)
    before = (chip[:, None] == chip[None, :]) & (partner[None, :] < partner[:, None])
    take_rank = jnp.sum(before, axis=1, dtype=jnp.int32)
    scale = vir_pair[None, :] - occ_pair[:, None]

    def send_place(wanted, rank, turn):
        to = wanted // row_count
        inside = (rank // SLOTS == turn) & (to % core_size == core)
        return to // core_size * STRIDE + jnp.where(inside, rank % SLOTS, SLOTS)

    packed = pltpu.VMEM((device_count // core_size * STRIDE, 2, width // 2), jnp.float32)
    chips = ("zh", "x", "y", "zl")

    def exchange(turn):
        outbox = pl.pallas_call(
            pack_kernel,
            in_specs=[SMEM, SMEM, SMEM, VMEM, VMEM],
            out_specs=VMEM,
            out_shape=packed,
            compiler_params=SMALL,
        )(send_place(partner, ranks[0], turn), send_place(sibling, ranks[1], turn), most, own, other)
        return in_vmem(lax.all_to_all(outbox, chips, 0, 0, tiled=True))

    update, turns = pl.pallas_call(
        unpack_kernel,
        in_specs=[SMEM, VMEM, VMEM, VMEM],
        out_specs=[VMEM, SMEM],
        out_shape=[jax.ShapeDtypeStruct((row_count, width), jnp.float32), pltpu.SMEM((1,), jnp.int32)],
        scratch_shapes=[pltpu.VMEM((row_count, width), jnp.float32)],
        compiler_params=SMALL,
    )(chip * STRIDE + take_rank % SLOTS, exchange(0), own, scale)

    def more(state):
        return state[0] < turns[0]

    def again(state):
        turn, so_far = state
        place = jnp.where(take_rank // SLOTS == turn, chip * STRIDE + take_rank % SLOTS, -1)
        after = pl.pallas_call(
            mend_kernel,
            in_specs=[SMEM, VMEM, VMEM, VMEM, VMEM],
            out_specs=VMEM,
            out_shape=jax.ShapeDtypeStruct((row_count, width), jnp.float32),
            compiler_params=SMALL,
        )(place, exchange(turn), own, scale, so_far)
        return turn + 1, after

    return lax.while_loop(more, again, (jnp.int32(1), update))[1]


def solution(mesh):
    fine = Mesh(mesh.devices.reshape(2, 4, 4, 2, 2), ("zh", "x", "y", "zl", "c"))
    ij, vir = ("zh", "x"), ("y", "zl", "c")
    in_specs = (
        P(ij, vir),
        P(vir + ij, None, None),
        P(vir + ij, None),
        P(ij + vir),
        P(ij + vir),
        P(),
    )
    return jax.shard_map(
        on_device, mesh=fine, in_specs=in_specs, out_specs=P(ij + vir, None), check_vma=False
    )
```

```python
import functools

import jax
import jax.numpy as jnp
from jax import lax
from jax.experimental import pallas as pl
from jax.experimental.pallas import tpu as pltpu
from jax.sharding import Mesh
from jax.sharding import PartitionSpec as P

SLOTS = 12
STRIDE = SLOTS + 1
SMEM = pl.BlockSpec(memory_space=pltpu.SMEM)
VMEM = pl.BlockSpec(memory_space=pltpu.VMEM)
HBM = pl.BlockSpec(memory_space=pltpu.HBM)
SMALL = pltpu.CompilerParams(vmem_limit_bytes=12 * 2**20)


def in_vmem(array):
    return pltpu.with_memory_space_constraint(array, pltpu.VMEM)


def in_hbm(array):
    return pltpu.with_memory_space_constraint(array, pltpu.HBM)


def split_bf16(values):
    high = values.astype(jnp.bfloat16)
    low = (values - high.astype(jnp.float32)).astype(jnp.bfloat16)
    return high, low


def halves_of(block):
    high, low = split_bf16(block)
    return [low, high, high]


def strips_of(rows, width):
    high, low = split_bf16(rows.reshape(-1, width))
    return [high, low, high]


def product(strips, right):
    return jnp.dot(jnp.concatenate(strips, axis=1), right, preferred_element_type=jnp.float32)


def columns_of(place, deep):
    return pl.ds(pl.multiple_of(place * deep, deep), deep)


def bring(far, near, side, arrived):
    step = far.shape[0] // arrived.shape[0]
    wide = near.shape[3]
    copies = []
    for n in range(arrived.shape[0]):
        part = pl.ds(n * step, step)
        source = far.at[part, :, :, columns_of(side, wide)]
        copies.append(pltpu.make_async_copy(source, near.at[part], arrived.at[n]))
        copies[-1].start()
    return step, copies


def both_cores(near, places, rows, column, deep):
    columns = columns_of(column, deep)
    return jnp.concatenate(
        [near[rows, places[half], :, columns].reshape(-1, deep) for half in range(2)]
    )


def first_kernel(places, block, far, near, out, arrived):
    deep, width = block.shape
    step, copies = bring(far, near, places[2], arrived)
    right = jnp.concatenate(halves_of(block[...]), axis=0)
    for n, copy in enumerate(copies):
        copy.wait()
        rows = slice(n * step, (n + 1) * step)
        strips = strips_of(both_cores(near, places, rows, places[4], deep), deep)
        out[:, rows] = product(strips, right).reshape(2, step, -1, width)


def second_kernel(places, here, left, right, across, totals, far, near, out, arrived):
    deep, width = across.shape
    step, copies = bring(far, near, places[3], arrived)
    sides = jnp.concatenate(halves_of(left[...]) + halves_of(right[...]), axis=0)
    for n in range(len(copies)):
        rows = slice(n * step, (n + 1) * step)
        strips = []
        for column in (places[5], places[6]):
            strips += strips_of(both_cores(here, places, rows, column, deep), deep)
        out[:, rows] = totals[:, rows] + product(strips, sides).reshape(2, step, -1, width)
    beyond = jnp.concatenate(halves_of(across[...]), axis=0)
    for n, copy in enumerate(copies):
        copy.wait()
        rows = slice(n * step, (n + 1) * step)
        strips = strips_of(both_cores(near, places, rows, places[4], deep), deep)
        out[:, rows] += product(strips, beyond).reshape(2, step, -1, width)


def last_kernel(half, places, here, there, far, across_left, across_right, across_far, totals, out):
    deep, width = far.shape
    blocks = (
        (here, places[7], far),
        (there, places[5], across_left),
        (there, places[6], across_right),
        (there, places[7], across_far),
    )
    right = jnp.concatenate(sum((halves_of(block[...]) for _, _, block in blocks), []), axis=0)
    step = 4
    for n in range(here.shape[0] // step):
        rows = slice(n * step, (n + 1) * step)
        strips = []
        for near, column, _ in blocks:
            strips += strips_of(near[rows, places[half], :, columns_of(column, deep)], deep)
        out[rows] = totals[half, rows] + product(strips, right).reshape(step, -1, width)


def call(kernel, operands, specs, results, scratch=(), aliases={}, flops=0):
    return pl.pallas_call(
        kernel,
        in_specs=specs,
        out_specs=[VMEM] * len(results),
        out_shape=[pltpu.VMEM(shape, jnp.float32) for shape in results],
        scratch_shapes=scratch,
        input_output_aliases=aliases,
        cost_estimate=pl.CostEstimate(flops=flops, bytes_accessed=2**20, transcendentals=0),
        compiler_params=SMALL,
    )(*operands)


def mask_kernel(mask, block, out, flags, held, arrived):
    copies = [
        pltpu.make_async_copy(mask, flags, arrived.at[0]),
        pltpu.make_async_copy(block, held, arrived.at[1]),
    ]
    for copy in copies:
        copy.start()
    for copy in copies:
        copy.wait()
    tiles, tile, width = block.shape
    for t in range(tiles):
        for a in range(mask.shape[1]):
            lanes = slice(a * tile, (a + 1) * tile)
            out[t * tile : (t + 1) * tile, lanes] = held[t, :, lanes] * flags[t, a].astype(jnp.float32)


def add_kernel(places, left, right, *outs):
    for n, out in enumerate(outs):
        out[...] = left[places[8 + n]] + right[places[8 + n]]


def sum_kernel(*refs):
    *parts, out = refs
    out[...] = sum(part[...] for part in parts)


def pack_kernel(own_place, other_place, most, own, other, out):
    rows = own.shape[0]
    half = own.shape[1] // 2
    for place, source in ((own_place, own), (other_place, other)):
        for k in range(rows):
            to = place[k]
            out[to, 0:1, :] = source[k : k + 1, :half]
            out[to, 1:2, :] = source[k : k + 1, half:]
    mark = jnp.full((2, half), most[0].astype(jnp.float32))
    for d in range(out.shape[0] // STRIDE):
        out[d * STRIDE + SLOTS] = mark


def unpack_kernel(place, got, own, scale, out, turns, held):
    half = own.shape[1] // 2
    for k in range(own.shape[0]):
        at = place[k]
        held[k : k + 1, :half] = got[at, 0:1, :]
        held[k : k + 1, half:] = got[at, 1:2, :]
    worst = jnp.zeros((2, half), jnp.float32)
    for d in range(got.shape[0] // STRIDE):
        worst = jnp.maximum(worst, got[d * STRIDE + SLOTS])
    turns[0] = (jnp.max(worst).astype(jnp.int32) + SLOTS - 1) // SLOTS
    out[...] = (own[...] - held[...]) / scale[...]


def mend_kernel(place, got, own, scale, before, out):
    half = own.shape[1] // 2
    for k in range(own.shape[0]):
        at = place[k]
        row = slice(k, k + 1)
        for part, lanes in enumerate((slice(0, half), slice(half, 2 * half))):
            fresh = (own[row, lanes] - got[jnp.maximum(at, 0), part : part + 1, :]) / scale[row, lanes]
            out[row, lanes] = jnp.where(at >= 0, fresh, before[row, lanes])


def on_device(amplitudes, integrals, block_mask, partner, occ_pair, vir_pair):
    tiles, tile, width = integrals.shape
    row_count = partner.shape[0]
    z_size, x_size, y_size, zl_size, core_size = (lax.axis_size(a) for a in ("zh", "x", "y", "zl", "c"))
    device_count = z_size * x_size * y_size * zl_size * core_size
    zh, x, core = lax.axis_index("zh"), lax.axis_index("x"), lax.axis_index("c")

    mine = pl.pallas_call(
        mask_kernel,
        in_specs=[HBM, HBM],
        out_specs=VMEM,
        out_shape=pltpu.VMEM((tiles * tile, width), jnp.float32),
        scratch_shapes=[
            pltpu.SMEM(block_mask.shape, jnp.int32),
            pltpu.VMEM(integrals.shape, jnp.float32),
            pltpu.SemaphoreType.DMA((2,)),
        ],
        compiler_params=SMALL,
    )(in_hbm(block_mask), in_hbm(integrals))

    def shift(block, by):
        return lax.ppermute(block, "x", [(n, (n + by) % x_size) for n in range(x_size)])

    def cross(block):
        return lax.ppermute(block, "zh", [(0, 1), (1, 0)])

    def swap(array):
        return lax.ppermute(array, "c", [(0, 1), (1, 0)])

    amps = amplitudes.reshape(y_size * zl_size, core_size, row_count, amplitudes.shape[1])

    left, right, opposite = (x + x_size - 1) % x_size, (x + 1) % x_size, (x + 2) % x_size
    where = [1 - core, core, zh, 1 - zh, x, left, right, opposite]
    y, zl = lax.axis_index("y"), lax.axis_index("zl")
    moves = [(1, 1), (3, 1), (2, 1), (2, 0), (0, 1), (1, 0), (3, 0), (0, 0)]
    where += [(y + up) % y_size * zl_size + (zl + over) % zl_size for up, over in moves]
    slot = jnp.arange(len(where), dtype=jnp.int32)
    places = jnp.zeros((len(where),), jnp.int32)
    for n, place in enumerate(where):
        places = jnp.where(slot == n, place.astype(jnp.int32), places)

    chunks = y_size * zl_size
    wide = amplitudes.shape[1] // z_size
    side = (chunks, core_size, row_count, wide)
    sums = (core_size, chunks, row_count, width)
    loads = [pltpu.SemaphoreType.DMA((4,))]
    work = 6 * core_size * chunks * row_count * width * tiles * tile

    across, up1, down1 = cross(mine), shift(mine, 1), shift(mine, -1)
    around = [(n, (1 - n // x_size) * x_size + (n + 2) % x_size) for n in range(2 * x_size)]
    across_far = lax.ppermute(mine, ("zh", "x"), around)
    here, total = call(
        first_kernel,
        [places, mine, in_hbm(amps)],
        [SMEM, VMEM, HBM],
        [side, sums],
        loads,
        flops=work,
    )
    across, up1, total = lax.optimization_barrier((across, up1, total))
    across_down1 = shift(across, -1)
    up2 = shift(up1, 1)
    across_up1 = cross(up1)
    there, total = call(
        second_kernel,
        [places, here, in_vmem(up1), in_vmem(down1), in_vmem(across), total, in_hbm(amps)],
        [SMEM, VMEM, VMEM, VMEM, VMEM, VMEM, HBM],
        [side, sums],
        loads,
        {5: 1},
        3 * work,
    )
    blocks = [in_vmem(block) for block in (up2, across_up1, across_down1, across_far)]

    def finish(half):
        (out,) = call(
            functools.partial(last_kernel, half),
            [places, here, there, *blocks, total],
            [SMEM] + [VMEM] * 7,
            [sums[1:]],
            flops=2 * work,
        )
        return out

    incoming = swap(finish(0))
    parts = call(
        add_kernel,
        [places, finish(1), in_vmem(incoming)],
        [SMEM, VMEM, VMEM],
        [sums[2:]] * len(moves),
    )

    def send(part, move):
        up, over = move
        pairs = [
            (a * zl_size + b, (a + up) % y_size * zl_size + (b + over) % zl_size)
            for a in range(y_size)
            for b in range(zl_size)
        ]
        return in_vmem(lax.ppermute(part, ("y", "zl"), pairs))

    partials = [send(part, move) for part, move in zip(parts[:-1], moves)] + [parts[-1]]
    partials[0], partner, core = lax.optimization_barrier((partials[0], partner, core))

    sibling = swap(partner)
    row = jnp.arange(row_count, dtype=jnp.int32)

    def rank(wanted, others, others_first):
        to, beside = wanted // row_count, others // row_count
        earlier = (to[:, None] == to[None, :]) & (row[None, :] < row[:, None])
        also = (to[:, None] == beside[None, :]) & others_first
        return jnp.sum(earlier.astype(jnp.int32) + also.astype(jnp.int32), axis=1)

    ranks = (rank(partner, sibling, core == 1), rank(sibling, partner, core == 0))
    most = (jnp.maximum(jnp.max(ranks[0]), jnp.max(ranks[1])) + 1).reshape(1)
    chip = partner // (row_count * core_size)
    before = (chip[:, None] == chip[None, :]) & (partner[None, :] < partner[:, None])
    take_rank = jnp.sum(before, axis=1, dtype=jnp.int32)
    scale = vir_pair[None, :] - occ_pair[:, None]

    def send_place(wanted, rank, turn):
        to = wanted // row_count
        inside = (rank // SLOTS == turn) & (to % core_size == core)
        return to // core_size * STRIDE + jnp.where(inside, rank % SLOTS, SLOTS)

    first = (send_place(partner, ranks[0], 0), send_place(sibling, ranks[1], 0), most)
    take_first = chip * STRIDE + take_rank % SLOTS
    partials[1], first, take_first, scale = lax.optimization_barrier(
        (partials[1], first, take_first, scale)
    )
    rows = pltpu.VMEM((row_count, width), jnp.float32)
    own = pl.pallas_call(
        sum_kernel,
        in_specs=[VMEM] * len(partials),
        out_specs=VMEM,
        out_shape=rows,
        compiler_params=SMALL,
    )(*partials)
    other = swap(own)

    packed = pltpu.VMEM((device_count // core_size * STRIDE, 2, width // 2), jnp.float32)
    chips = ("zh", "x", "y", "zl")

    def exchange(places):
        outbox = pl.pallas_call(
            pack_kernel,
            in_specs=[SMEM, SMEM, SMEM, VMEM, VMEM],
            out_specs=VMEM,
            out_shape=packed,
            compiler_params=SMALL,
        )(*places, own, other)
        return in_vmem(lax.all_to_all(outbox, chips, 0, 0, tiled=True))

    update, turns = pl.pallas_call(
        unpack_kernel,
        in_specs=[SMEM, VMEM, VMEM, VMEM],
        out_specs=[VMEM, SMEM],
        out_shape=[jax.ShapeDtypeStruct((row_count, width), jnp.float32), pltpu.SMEM((1,), jnp.int32)],
        scratch_shapes=[pltpu.VMEM((row_count, width), jnp.float32)],
        compiler_params=SMALL,
    )(take_first, exchange(first), own, scale)

    def more(state):
        return state[0] < turns[0]

    def again(state):
        turn, so_far = state
        to_places = (send_place(partner, ranks[0], turn), send_place(sibling, ranks[1], turn), most)
        place = jnp.where(take_rank // SLOTS == turn, chip * STRIDE + take_rank % SLOTS, -1)
        after = pl.pallas_call(
            mend_kernel,
            in_specs=[SMEM, VMEM, VMEM, VMEM, VMEM],
            out_specs=VMEM,
            out_shape=jax.ShapeDtypeStruct((row_count, width), jnp.float32),
            compiler_params=SMALL,
        )(place, exchange(to_places), own, scale, so_far)
        return turn + 1, after

    return lax.while_loop(more, again, (jnp.int32(1), update))[1]


def solution(mesh):
    fine = Mesh(mesh.devices.reshape(2, 4, 4, 2, 2), ("zh", "x", "y", "zl", "c"))
    ij, vir = ("zh", "x"), ("y", "zl", "c")
    in_specs = (
        P(ij, vir),
        P(vir + ij, None, None),
        P(vir + ij, None),
        P(ij + vir),
        P(ij + vir),
        P(),
    )
    return jax.shard_map(
        on_device, mesh=fine, in_specs=in_specs, out_specs=P(ij + vir, None), check_vma=False
    )
```

```python
import functools

import jax
import jax.numpy as jnp
from jax import lax
from jax.experimental import pallas as pl
from jax.experimental.pallas import tpu as pltpu
from jax.sharding import Mesh
from jax.sharding import PartitionSpec as P

SLOTS = 12
STRIDE = SLOTS + 1
SMEM = pl.BlockSpec(memory_space=pltpu.SMEM)
VMEM = pl.BlockSpec(memory_space=pltpu.VMEM)
HBM = pl.BlockSpec(memory_space=pltpu.HBM)
SMALL = pltpu.CompilerParams(vmem_limit_bytes=12 * 2**20)


def in_vmem(array):
    return pltpu.with_memory_space_constraint(array, pltpu.VMEM)


def in_hbm(array):
    return pltpu.with_memory_space_constraint(array, pltpu.HBM)


def split_bf16(values):
    high = values.astype(jnp.bfloat16)
    low = (values - high.astype(jnp.float32)).astype(jnp.bfloat16)
    return high, low


def halves_of(block):
    high, low = split_bf16(block)
    return [low, high, high]


def strips_of(rows, width):
    high, low = split_bf16(rows.reshape(-1, width))
    return [high, low, high]


def product(strips, right):
    return jnp.dot(jnp.concatenate(strips, axis=1), right, preferred_element_type=jnp.float32)


def columns_of(place, deep):
    return pl.ds(pl.multiple_of(place * deep, deep), deep)


def bring(far, near, side, arrived):
    step = far.shape[0] // arrived.shape[0]
    wide = near.shape[3]
    copies = []
    for n in range(arrived.shape[0]):
        part = pl.ds(n * step, step)
        source = far.at[part, :, :, columns_of(side, wide)]
        copies.append(pltpu.make_async_copy(source, near.at[part], arrived.at[n]))
        copies[-1].start()
    return step, copies


def both_cores(near, places, rows, column, deep):
    columns = columns_of(column, deep)
    return jnp.concatenate(
        [near[rows, places[half], :, columns].reshape(-1, deep) for half in range(2)]
    )


def first_kernel(places, block, far, near, out, arrived):
    deep, width = block.shape
    step, copies = bring(far, near, places[2], arrived)
    right = jnp.concatenate(halves_of(block[...]), axis=0)
    for n, copy in enumerate(copies):
        copy.wait()
        rows = slice(n * step, (n + 1) * step)
        strips = strips_of(both_cores(near, places, rows, places[4], deep), deep)
        out[:, rows] = product(strips, right).reshape(2, step, -1, width)


def second_kernel(places, here, left, right, across, totals, far, near, out, arrived):
    deep, width = across.shape
    step, copies = bring(far, near, places[3], arrived)
    sides = jnp.concatenate(halves_of(left[...]) + halves_of(right[...]), axis=0)
    for n in range(len(copies)):
        rows = slice(n * step, (n + 1) * step)
        strips = []
        for column in (places[5], places[6]):
            strips += strips_of(both_cores(here, places, rows, column, deep), deep)
        out[:, rows] = totals[:, rows] + product(strips, sides).reshape(2, step, -1, width)
    beyond = jnp.concatenate(halves_of(across[...]), axis=0)
    for n, copy in enumerate(copies):
        copy.wait()
        rows = slice(n * step, (n + 1) * step)
        strips = strips_of(both_cores(near, places, rows, places[4], deep), deep)
        out[:, rows] += product(strips, beyond).reshape(2, step, -1, width)


def last_kernel(half, places, here, there, far, across_left, across_right, across_far, totals, out):
    deep, width = far.shape
    blocks = (
        (here, places[7], far),
        (there, places[5], across_left),
        (there, places[6], across_right),
        (there, places[7], across_far),
    )
    right = jnp.concatenate(sum((halves_of(block[...]) for _, _, block in blocks), []), axis=0)
    step = 4
    for n in range(here.shape[0] // step):
        rows = slice(n * step, (n + 1) * step)
        strips = []
        for near, column, _ in blocks:
            strips += strips_of(near[rows, places[half], :, columns_of(column, deep)], deep)
        out[rows] = totals[half, rows] + product(strips, right).reshape(step, -1, width)


def call(kernel, operands, specs, results, scratch=(), aliases={}, flops=0):
    return pl.pallas_call(
        kernel,
        in_specs=specs,
        out_specs=[VMEM] * len(results),
        out_shape=[pltpu.VMEM(shape, jnp.float32) for shape in results],
        scratch_shapes=scratch,
        input_output_aliases=aliases,
        cost_estimate=pl.CostEstimate(flops=flops, bytes_accessed=2**20, transcendentals=0),
        compiler_params=SMALL,
    )(*operands)


def mask_kernel(mask, block, out, flags, held, arrived):
    copies = [
        pltpu.make_async_copy(mask, flags, arrived.at[0]),
        pltpu.make_async_copy(block, held, arrived.at[1]),
    ]
    for copy in copies:
        copy.start()
    for copy in copies:
        copy.wait()
    tiles, tile, width = block.shape
    for t in range(tiles):
        for a in range(mask.shape[1]):
            lanes = slice(a * tile, (a + 1) * tile)
            out[t * tile : (t + 1) * tile, lanes] = held[t, :, lanes] * flags[t, a].astype(jnp.float32)


def add_kernel(places, left, right, *outs):
    for n, out in enumerate(outs):
        out[...] = left[places[8 + n]] + right[places[8 + n]]


def sum_kernel(*refs):
    *parts, out = refs
    out[...] = sum(part[...] for part in parts)


def pack_kernel(own_place, other_place, most, own, other, out):
    rows = own.shape[0]
    half = own.shape[1] // 2
    for place, source in ((own_place, own), (other_place, other)):
        for k in range(rows):
            to = place[k]
            out[to, 0:1, :] = source[k : k + 1, :half]
            out[to, 1:2, :] = source[k : k + 1, half:]
    mark = jnp.full((2, half), most[0].astype(jnp.float32))
    for d in range(out.shape[0] // STRIDE):
        out[d * STRIDE + SLOTS] = mark


def unpack_kernel(place, got, own, scale, out, turns, held):
    half = own.shape[1] // 2
    for k in range(own.shape[0]):
        at = place[k]
        held[k : k + 1, :half] = got[at, 0:1, :]
        held[k : k + 1, half:] = got[at, 1:2, :]
    worst = jnp.zeros((2, half), jnp.float32)
    for d in range(got.shape[0] // STRIDE):
        worst = jnp.maximum(worst, got[d * STRIDE + SLOTS])
    turns[0] = (jnp.max(worst).astype(jnp.int32) + SLOTS - 1) // SLOTS
    out[...] = (own[...] - held[...]) / scale[...]


def mend_kernel(place, got, own, scale, before, out):
    half = own.shape[1] // 2
    for k in range(own.shape[0]):
        at = place[k]
        row = slice(k, k + 1)
        for part, lanes in enumerate((slice(0, half), slice(half, 2 * half))):
            fresh = (own[row, lanes] - got[jnp.maximum(at, 0), part : part + 1, :]) / scale[row, lanes]
            out[row, lanes] = jnp.where(at >= 0, fresh, before[row, lanes])


def on_device(amplitudes, integrals, block_mask, partner, occ_pair, vir_pair):
    tiles, tile, width = integrals.shape
    row_count = partner.shape[0]
    z_size, x_size, y_size, zl_size, core_size = (lax.axis_size(a) for a in ("zh", "x", "y", "zl", "c"))
    device_count = z_size * x_size * y_size * zl_size * core_size
    zh, x, core = lax.axis_index("zh"), lax.axis_index("x"), lax.axis_index("c")

    mine = pl.pallas_call(
        mask_kernel,
        in_specs=[HBM, HBM],
        out_specs=VMEM,
        out_shape=pltpu.VMEM((tiles * tile, width), jnp.float32),
        scratch_shapes=[
            pltpu.SMEM(block_mask.shape, jnp.int32),
            pltpu.VMEM(integrals.shape, jnp.float32),
            pltpu.SemaphoreType.DMA((2,)),
        ],
        compiler_params=SMALL,
    )(in_hbm(block_mask), in_hbm(integrals))

    def shift(block, by):
        return lax.ppermute(block, "x", [(n, (n + by) % x_size) for n in range(x_size)])

    def cross(block):
        return lax.ppermute(block, "zh", [(0, 1), (1, 0)])

    def swap(array):
        return lax.ppermute(array, "c", [(0, 1), (1, 0)])

    amps = amplitudes.reshape(y_size * zl_size, core_size, row_count, amplitudes.shape[1])

    left, right, opposite = (x + x_size - 1) % x_size, (x + 1) % x_size, (x + 2) % x_size
    where = [1 - core, core, zh, 1 - zh, x, left, right, opposite]
    y, zl = lax.axis_index("y"), lax.axis_index("zl")
    moves = [(1, 1), (3, 1), (1, 0), (3, 0), (2, 1), (2, 0), (0, 1), (0, 0)]
    where += [(y + up) % y_size * zl_size + (zl + over) % zl_size for up, over in moves]
    slot = jnp.arange(len(where), dtype=jnp.int32)
    places = jnp.zeros((len(where),), jnp.int32)
    for n, place in enumerate(where):
        places = jnp.where(slot == n, place.astype(jnp.int32), places)

    chunks = y_size * zl_size
    wide = amplitudes.shape[1] // z_size
    side = (chunks, core_size, row_count, wide)
    sums = (core_size, chunks, row_count, width)
    loads = [pltpu.SemaphoreType.DMA((8,))]
    work = 6 * core_size * chunks * row_count * width * tiles * tile

    across, up1, down1 = cross(mine), shift(mine, 1), shift(mine, -1)
    around = [(n, (1 - n // x_size) * x_size + (n + 2) % x_size) for n in range(2 * x_size)]
    across_far = lax.ppermute(mine, ("zh", "x"), around)
    here, total = call(
        first_kernel,
        [places, mine, in_hbm(amps)],
        [SMEM, VMEM, HBM],
        [side, sums],
        loads,
        flops=work,
    )
    across, up1, total = lax.optimization_barrier((across, up1, total))
    across_down1 = shift(across, -1)
    up2 = shift(up1, 1)
    across_up1 = cross(up1)
    there, total = call(
        second_kernel,
        [places, here, in_vmem(up1), in_vmem(down1), in_vmem(across), total, in_hbm(amps)],
        [SMEM, VMEM, VMEM, VMEM, VMEM, VMEM, HBM],
        [side, sums],
        loads,
        {5: 1},
        3 * work,
    )
    blocks = [in_vmem(block) for block in (up2, across_up1, across_down1, across_far)]

    def finish(half):
        (out,) = call(
            functools.partial(last_kernel, half),
            [places, here, there, *blocks, total],
            [SMEM] + [VMEM] * 7,
            [sums[1:]],
            flops=2 * work,
        )
        return out

    incoming = swap(finish(0))
    parts = call(
        add_kernel,
        [places, finish(1), in_vmem(incoming)],
        [SMEM, VMEM, VMEM],
        [sums[2:]] * len(moves),
    )

    def send(part, move):
        up, over = move
        pairs = [
            (a * zl_size + b, (a + up) % y_size * zl_size + (b + over) % zl_size)
            for a in range(y_size)
            for b in range(zl_size)
        ]
        return in_vmem(lax.ppermute(part, ("y", "zl"), pairs))

    partials = [send(part, move) for part, move in zip(parts[:-1], moves)] + [parts[-1]]
    partials[0], partner, core = lax.optimization_barrier((partials[0], partner, core))

    sibling = swap(partner)
    row = jnp.arange(row_count, dtype=jnp.int32)

    def rank(wanted, others, others_first):
        to, beside = wanted // row_count, others // row_count
        earlier = (to[:, None] == to[None, :]) & (row[None, :] < row[:, None])
        also = (to[:, None] == beside[None, :]) & others_first
        return jnp.sum(earlier.astype(jnp.int32) + also.astype(jnp.int32), axis=1)

    ranks = (rank(partner, sibling, core == 1), rank(sibling, partner, core == 0))
    most = (jnp.maximum(jnp.max(ranks[0]), jnp.max(ranks[1])) + 1).reshape(1)
    chip = partner // (row_count * core_size)
    before = (chip[:, None] == chip[None, :]) & (partner[None, :] < partner[:, None])
    take_rank = jnp.sum(before, axis=1, dtype=jnp.int32)
    scale = vir_pair[None, :] - occ_pair[:, None]

    def send_place(wanted, rank, turn):
        to = wanted // row_count
        inside = (rank // SLOTS == turn) & (to % core_size == core)
        return to // core_size * STRIDE + jnp.where(inside, rank % SLOTS, SLOTS)

    first = (send_place(partner, ranks[0], 0), send_place(sibling, ranks[1], 0), most)
    take_first = chip * STRIDE + take_rank % SLOTS
    partials[1], first, take_first, scale = lax.optimization_barrier(
        (partials[1], first, take_first, scale)
    )
    rows = pltpu.VMEM((row_count, width), jnp.float32)
    own = pl.pallas_call(
        sum_kernel,
        in_specs=[VMEM] * len(partials),
        out_specs=VMEM,
        out_shape=rows,
        compiler_params=SMALL,
    )(*partials)
    other = swap(own)

    packed = pltpu.VMEM((device_count // core_size * STRIDE, 2, width // 2), jnp.float32)
    chips = ("zh", "x", "y", "zl")

    def exchange(places):
        outbox = pl.pallas_call(
            pack_kernel,
            in_specs=[SMEM, SMEM, SMEM, VMEM, VMEM],
            out_specs=VMEM,
            out_shape=packed,
            compiler_params=SMALL,
        )(*places, own, other)
        return in_vmem(lax.all_to_all(outbox, chips, 0, 0, tiled=True))

    update, turns = pl.pallas_call(
        unpack_kernel,
        in_specs=[SMEM, VMEM, VMEM, VMEM],
        out_specs=[VMEM, SMEM],
        out_shape=[jax.ShapeDtypeStruct((row_count, width), jnp.float32), pltpu.SMEM((1,), jnp.int32)],
        scratch_shapes=[pltpu.VMEM((row_count, width), jnp.float32)],
        compiler_params=SMALL,
    )(take_first, exchange(first), own, scale)

    def more(state):
        return state[0] < turns[0]

    def again(state):
        turn, so_far = state
        to_places = (send_place(partner, ranks[0], turn), send_place(sibling, ranks[1], turn), most)
        place = jnp.where(take_rank // SLOTS == turn, chip * STRIDE + take_rank % SLOTS, -1)
        after = pl.pallas_call(
            mend_kernel,
            in_specs=[SMEM, VMEM, VMEM, VMEM, VMEM],
            out_specs=VMEM,
            out_shape=jax.ShapeDtypeStruct((row_count, width), jnp.float32),
            compiler_params=SMALL,
        )(place, exchange(to_places), own, scale, so_far)
        return turn + 1, after

    return lax.while_loop(more, again, (jnp.int32(1), update))[1]


def solution(mesh):
    fine = Mesh(mesh.devices.reshape(2, 4, 4, 2, 2), ("zh", "x", "y", "zl", "c"))
    ij, vir = ("zh", "x"), ("y", "zl", "c")
    in_specs = (
        P(ij, vir),
        P(vir + ij, None, None),
        P(vir + ij, None),
        P(ij + vir),
        P(ij + vir),
        P(),
    )
    return jax.shard_map(
        on_device, mesh=fine, in_specs=in_specs, out_specs=P(ij + vir, None), check_vma=False
    )
```
